32 devices in a mesh: wide: 8 (over z, y), quad: 4 (over x, core).
Axes of the slice: x: 2, y: 2, z: 4, core: 2. Of those that a mesh axis runs over, the one named last changes fastest.
Arguments:
- orbitals: float32 [16, 64, 4096], P('wide', 'quad'), may hold values from -6 to 6
- corners: int32 [16, 2], P('wide'), may hold values from 0 to 16
- pair_partner: int32 [32], P('wide'), may hold values from 0 to 15, as said below
- pair_live: int32 [32], P('wide'), may hold values from 0 to 1, as said below
Outputs:
- exchange_action: float32 [16, 64, 4096], P('wide', 'quad')
The draws below stay inside these ranges and needn't reach their ends.
Inputs may be any that keep to these rules, and one draw needn't show every extreme that they name: For the slots of owner w, the second orbital lies between the first plus 1 and the first plus 4 where the slot is live; every pair_partner is a valid orbital index. The number of live slots differs from owner to owner, and owner 0 has all 4 live. `pair_live`: dead slots may stand anywhere among an owner's slots.
All inputs are finite; a program needn't handle non-finite values.
Results may differ from the reference program's by a relative error of at most 0.0003.
Values sent between devices are 32-bit elements; how exact they have to be, the bound alone decides.
A program may use at most 64 MiB of HBM per device.

```python
import math
import jax
import jax.numpy as jnp
from jax import lax

BX = 64
BY = 64
BZ = 64
SPAN = 16
ORB_DEV = 2
PAIR_DEV = 4
SWEEPS = 8
REACH = 4
ORB = 16
PAIRS = 32


def pair_tables(key):
    slots = jnp.arange(PAIRS, dtype=jnp.int32)
    owner = slots // PAIR_DEV
    within = slots % PAIR_DEV
    first = owner * ORB_DEV + within % ORB_DEV
    delta = jax.random.randint(jax.random.fold_in(key, 7), (PAIRS,), 1, REACH + 1)
    counts = jax.random.randint(jax.random.fold_in(key, 8), (PAIRS // PAIR_DEV,), 2, PAIR_DEV + 1)
    counts = counts.at[0].set(PAIR_DEV)
    second = first + delta
    live = (within < counts[owner]) & (second < ORB)
    second = jnp.minimum(second, ORB - 1)
    return (second.astype(jnp.int32), live.astype(jnp.int32))


def draw_pair_partner(key, part):
    return pair_tables(key)[0]


def draw_pair_live(key, part):
    return pair_tables(key)[1]


def set_ends(values, own_key, smallest, top_value):
    place = [jax.random.randint(jax.random.fold_in(own_key, axis), (), 0, length) for axis, length in enumerate(values.shape)]
    main_axis = values.shape.index(max(values.shape))
    next_to = place[:main_axis] + [(place[main_axis] + 1) % values.shape[main_axis]] + place[main_axis + 1:]
    return values.at[tuple(place)].set(smallest).at[tuple(next_to)].set(top_value)


def shard_levels(rng, extent, cuts, low, high):
    def one(dim, parts):
        heights = jax.random.uniform(jax.random.fold_in(jax.random.fold_in(rng, 6), dim), (parts,), jnp.float32, low / len(cuts), high / len(cuts))
        return jnp.repeat(jnp.exp(heights), extent[dim] // parts).reshape((-1,) + (1,) * (len(extent) - dim - 1))

    level = one(*cuts[0])
    for cut in cuts[1:]:
        level = level * one(*cut)
    return level


def normal_values(rng, dims, spread, most, shards=(), kind=jnp.bfloat16):
    gain = shard_levels(rng, dims, shards, -0.22, 0.18) if shards else 1.0
    values = jax.random.normal(rng, dims, jnp.float32) * spread * gain
    return jnp.minimum(jnp.maximum(values, -most), most).astype(kind)


def setup_inputs(seed: int = 0) -> dict:
    key_of = jax.random.split(jax.random.key(seed), 5)
    return {
        "orbitals": normal_values(key_of[0], (ORB, BX, BY * BZ), 1.0, 6.0, ((0, 8), (1, 4)), jnp.float32),
        "corners": set_ends(jax.random.randint(key_of[1], (ORB, 2), 0, SPAN + 1), jax.random.fold_in(key_of[1], 1), 0, SPAN).astype(jnp.int32),
        "pair_partner": draw_pair_partner(jax.random.fold_in(key_of[4], 71), 0),
        "pair_live": draw_pair_live(jax.random.fold_in(key_of[4], 71), 0),
    }


def sweep_weights():
    low = 0.5 / 6.5
    high = 12.5 / 6.5
    center = (high + low) / 2.0
    half = (high - low) / 2.0
    return [1.0 / (center + half * math.cos(math.pi * (2 * k + 1) / (2 * SWEEPS))) for k in range(SWEEPS)]


def move_box(box, shift_y, shift_z):
    margin = SPAN * BZ + SPAN
    flat = box.shape[-1]
    padded = jnp.pad(box, ((0, 0), (margin, margin)))
    start = (margin - shift_y * BZ - shift_z).astype(jnp.int32)
    taken = lax.dynamic_slice_in_dim(padded, start, flat, 1)
    source = jnp.arange(flat, dtype=jnp.int32) % BZ - shift_z
    keep = (source >= 0) & (source < BZ)
    return jnp.where(keep[None, :], taken, jnp.zeros_like(taken))


def neighbours(field, padded):
    flat = field.shape[-1]
    zpos = jnp.arange(flat, dtype=jnp.int32) % BZ
    total = padded[:, 2:] + padded[:, :-2]
    upper_z = jnp.pad(field[..., 1:], ((0, 0), (0, 0), (0, 1)))
    lower_z = jnp.pad(field[..., :-1], ((0, 0), (0, 0), (1, 0)))
    total = total + jnp.where(zpos < BZ - 1, upper_z, 0.0) + jnp.where(zpos > 0, lower_z, 0.0)
    total = total + jnp.pad(field[..., BZ:], ((0, 0), (0, 0), (0, BZ)))
    total = total + jnp.pad(field[..., :-BZ], ((0, 0), (0, 0), (BZ, 0)))
    return total


def solve_local(density):
    weights = sweep_weights()
    potential = weights[0] * density / 6.5
    for k in range(1, SWEEPS):
        padded = jnp.pad(potential, ((0, 0), (1, 1), (0, 0)))
        applied = 6.5 * potential - neighbours(potential, padded)
        potential = potential + weights[k] * (density - applied) / 6.5
    return potential


def reference(orbitals, corners, pair_partner, pair_live):
    slots = jnp.arange(PAIRS, dtype=jnp.int32)
    first = (slots // PAIR_DEV) * ORB_DEV + (slots % PAIR_DEV) % ORB_DEV

    def one_pair(total, item):
        left, right, live = item
        own = orbitals[left]
        offset = corners[right] - corners[left]
        moved = move_box(orbitals[right], offset[0], offset[1])
        density = own * moved * live.astype(jnp.float32)
        potential = solve_local(density[None])[0]
        total = total.at[left].add(potential * moved)
        total = total.at[right].add(move_box(potential * own, -offset[0], -offset[1]))
        return total, None

    start = jnp.zeros(orbitals.shape, jnp.float32)
    result, unused = lax.scan(one_pair, start, (first, pair_partner, pair_live))
    return result
```

```python
import functools
import math

import jax
import jax.numpy as jnp
from jax import lax
from jax.experimental import pallas as pl
from jax.experimental.pallas import tpu as pltpu
from jax.sharding import PartitionSpec as P

BZ = 64
SPAN = 16
SWEEPS = 8
REACH = 4
LANES = 128
EDGE = 8
LOW = 16
CHUNKS = 8
MESH = pl.DeviceIdType.MESH


def sweep_weights():
    low = 0.5 / 6.5
    high = 12.5 / 6.5
    center = (high + low) / 2.0
    half = (high - low) / 2.0
    return [
        1.0 / (center + half * math.cos(math.pi * (2 * k + 1) / (2 * SWEEPS)))
        for k in range(SWEEPS)
    ]


def remote(src, dst, send, recv, target):
    return pltpu.make_async_remote_copy(
        src_ref=src, dst_ref=dst, send_sem=send, recv_sem=recv,
        device_id=target, device_id_type=MESH,
    )


def enter(near):
    barrier = pltpu.get_barrier_semaphore()
    for there, target in near:
        @pl.when(there)
        def _(target=target):
            pl.semaphore_signal(barrier, inc=1, device_id=target, device_id_type=MESH)
    count = jnp.int32(0)
    for there, target in near:
        count = count + jnp.where(there, 1, 0)
    pl.semaphore_wait(barrier, count)


def gather_kernel(
    wides, quads, orb, corner_in, pool, corner,
    local_sem, corner_send, corner_recv, send_two, recv_two, send_one, recv_one,
    edge_send, edge_recv, own_send, own_recv,
):
    owned, planes, flat = orb.shape
    chunk_width = flat // CHUNKS
    w = lax.axis_index("wide")
    q = lax.axis_index("quad")
    odd = lax.rem(w, 2)
    is_odd = odd == 1
    is_even = odd == 0
    pair = w + 1 - 2 * odd
    has_one = jnp.logical_or(is_even, w + 1 < wides)
    has_two = w + 2 < wides
    gives_two = w >= 2
    below = q >= 1
    above = q + 1 < quads
    enter([
        (w >= 1, {"wide": w - 1}), (gives_two, {"wide": w - 2}),
        (w + 1 < wides, {"wide": w + 1}), (has_two, {"wide": w + 2}),
        (below, {"quad": q - 1}), (above, {"quad": q + 1}),
    ])

    def columns(c):
        return pl.ds(c * chunk_width, chunk_width)

    def held(step, c):
        return pool.at[pl.ds(step * owned, owned), pl.ds(EDGE, planes), columns(c)]

    def corner_copy(step):
        return remote(
            corner_in, corner.at[step], corner_send.at[step - 1], corner_recv.at[step - 1],
            {"wide": w - step},
        )

    def own_to_two(c):
        return remote(
            orb.at[:, :, columns(c)], held(2, c), send_two.at[c], recv_two.at[c],
            {"wide": w - 2},
        )

    def own_to_pair(c):
        return remote(
            orb.at[:, :, columns(c)], held(1, c), send_one.at[c], recv_one.at[c],
            {"wide": pair},
        )

    def two_to_pair(c):
        return remote(held(2, c), held(1, c), send_one.at[c], recv_one.at[c], {"wide": pair})

    def own_edge(up):
        if up:
            return remote(
                orb.at[:, pl.ds(planes - EDGE, EDGE)],
                pool.at[pl.ds(0, owned), pl.ds(0, EDGE)],
                own_send.at[1], own_recv.at[1], {"quad": q + 1},
            )
        return remote(
            orb.at[:, pl.ds(0, EDGE)],
            pool.at[pl.ds(0, owned), pl.ds(EDGE + planes, EDGE)],
            own_send.at[0], own_recv.at[0], {"quad": q - 1},
        )

    def edge(step, up, c):
        rows = pl.ds(step * owned, owned)
        if up:
            src, dst, to = planes, 0, q + 1
        else:
            src, dst, to = EDGE, EDGE + planes, q - 1
        return remote(
            pool.at[rows, pl.ds(src, EDGE), columns(c)],
            pool.at[rows, pl.ds(dst, EDGE), columns(c)],
            edge_send.at[step - 1, int(up), c], edge_recv.at[step - 1, int(up), c],
            {"quad": to},
        )

    own_copy = pltpu.make_async_copy(
        orb, pool.at[pl.ds(0, owned), pl.ds(EDGE, planes)], local_sem.at[0]
    )
    corner_copy_own = pltpu.make_async_copy(corner_in, corner.at[0], local_sem.at[1])
    for step in (1, 2):
        @pl.when(w >= step)
        def _(step=step):
            corner_copy(step).start()
    for c in range(CHUNKS):
        @pl.when(gives_two)
        def _(c=c):
            own_to_two(c).start()

        @pl.when(is_odd)
        def _(c=c):
            own_to_pair(c).start()

    @pl.when(below)
    def _():
        own_edge(False).start()

    @pl.when(above)
    def _():
        own_edge(True).start()
    own_copy.start()
    corner_copy_own.start()

    def pass_edges(step, c):
        @pl.when(below)
        def _():
            edge(step, False, c).start()

        @pl.when(above)
        def _():
            edge(step, True, c).start()

    for c in range(CHUNKS):
        @pl.when(has_two)
        def _(c=c):
            own_to_two(c).wait_recv()

            @pl.when(is_even)
            def _():
                two_to_pair(c).start()
            pass_edges(2, c)

        @pl.when(has_one)
        def _(c=c):
            own_to_pair(c).wait_recv()
            pass_edges(1, c)

    for up, takes, gives in ((False, above, below), (True, below, above)):
        @pl.when(takes)
        def _(up=up):
            own_edge(up).wait_recv()

        @pl.when(gives)
        def _(up=up):
            own_edge(up).wait_send()
        for step, have in ((2, has_two), (1, has_one)):
            for c in range(CHUNKS):
                @pl.when(jnp.logical_and(takes, have))
                def _(up=up, step=step, c=c):
                    edge(step, up, c).wait_recv()

                @pl.when(jnp.logical_and(gives, have))
                def _(up=up, step=step, c=c):
                    edge(step, up, c).wait_send()
    for step in (1, 2):
        @pl.when(w + step < wides)
        def _(step=step):
            corner_copy(step).wait_recv()

        @pl.when(w >= step)
        def _(step=step):
            corner_copy(step).wait_send()
    for c in range(CHUNKS):
        @pl.when(gives_two)
        def _(c=c):
            own_to_two(c).wait_send()

        @pl.when(jnp.logical_or(is_odd, has_two))
        def _(c=c):
            own_to_pair(c).wait_send()
    own_copy.wait()
    corner_copy_own.wait()


def exchange_kernel(
    quads, pool, corner_s, partner_ref, live_ref, seg, dens, moved, pot, final, prod,
):
    total_orbs, wide_rows, flat = pool.shape
    owned = total_orbs // 3
    planes = wide_rows - 2 * EDGE
    slots = partner_ref.shape[0]
    tiles = flat // LANES
    rows_y = flat // BZ
    w = lax.axis_index("wide")
    q = lax.axis_index("quad")

    zero_rows = jnp.zeros((dens.shape[2], LANES), jnp.float32)
    for s in range(slots):
        dens[s, 0] = zero_rows
        dens[s, tiles + 1] = zero_rows
    for b in range(2):
        pot[b, 0] = zero_rows
        pot[b, tiles + 1] = zero_rows

    lane = lax.broadcasted_iota(jnp.int32, (wide_rows, LANES), 1)
    zpos = lax.rem(lane, BZ)
    ylow = lane // BZ
    plane = lax.broadcasted_iota(jnp.int32, (wide_rows, LANES), 0) + (q * planes - EDGE)
    in_box = (plane >= 0) & (plane < quads * planes)

    def slot_facts(s):
        left = s % owned
        right = jnp.clip(partner_ref[s] - w * owned, 0, 3 * owned - 1)
        live = live_ref[s] != 0
        who, which = right // owned, lax.rem(right, owned)
        dy = corner_s[who, which, 0] - corner_s[0, left, 0]
        dz = corner_s[who, which, 1] - corner_s[0, left, 1]
        dy = jnp.clip(jnp.where(live, dy, 0), -SPAN, SPAN)
        dz = jnp.clip(jnp.where(live, dz, 0), -SPAN, SPAN)
        return left, right, live, dy, dz

    def mover(dy, dz, ok, rows):
        by = dy * BZ + dz
        whole = by >> 7
        rest = by & (LANES - 1)
        near_part = lane[:rows] < LANES - rest
        zfrom = zpos[:rows] - dz
        keep_z = (zfrom >= 0) & (zfrom < BZ) & ok
        yfrom = ylow[:rows] - dy

        def move(load, r):
            here = load(jnp.clip(r - whole, 0, tiles - 1))
            before = load(jnp.clip(r - whole - 1, 0, tiles - 1))
            turned = pltpu.roll(jnp.where(near_part, here, before), rest, 1)
            source = yfrom + 2 * r
            keep = keep_z & (source >= 0) & (source < rows_y)
            return jnp.where(keep, turned, 0.0)

        return move

    def column(t):
        return pl.ds(pl.multiple_of(t * LANES, LANES), LANES)

    facts = [slot_facts(s) for s in range(slots)]
    for s in range(slots):
        left, right, live, dy, dz = facts[s]
        move = mover(dy, dz, live, wide_rows)

        def one_tile(r, carry, s=s, left=left, right=right, move=move):
            there = move(lambda t: pool[right, :, column(t)], r)
            moved[s, r] = there[EDGE:EDGE + planes]
            dens[s, r + 1, LOW - EDGE:LOW + planes + EDGE] = jnp.where(
                in_box, there * pool[left, :, column(r)], 0.0
            )
            return carry

        lax.fori_loop(0, tiles, one_tile, 0, unroll=2)

    weights = sweep_weights()

    def stencil(read, r, first, size):
        upper = lane[:size] >= BZ
        v = read(r + 1, first, size)
        cross = v + jnp.where(upper, read(r, first, size), read(r + 2, first, size))
        total = read(r + 1, first + 1, size) + read(r + 1, first - 1, size)
        total = total + pltpu.roll(cross, BZ, 1)
        total = total + jnp.where(zpos[:size] > 0, pltpu.roll(v, 1, 1), 0.0)
        total = total + jnp.where(zpos[:size] < BZ - 1, pltpu.roll(v, LANES - 1, 1), 0.0)
        return v, total

    def one_slot(s, carry):
        for k in range(1, SWEEPS):
            gain = weights[k] / 6.5
            if k == 1:
                read = lambda t, first, size: dens[s, t, pl.ds(first, size)]
            else:
                read = lambda t, first, size, b=k % 2: pot[b, t, pl.ds(first, size)]
            last = k == SWEEPS - 1

            def one_tile(r, inner, k=k, gain=gain, read=read, last=last):
                first, size = (LOW, planes) if last else (LOW - EDGE, wide_rows)
                v, total = stencil(read, r, first, size)
                if k == 1:
                    start = weights[0] / 6.5
                    new = ((1.0 - weights[1]) * start + gain) * v + (gain * start) * total
                else:
                    d = dens[s, r + 1, pl.ds(first, size)]
                    new = (1.0 - weights[k]) * v + gain * (d + total)
                if last:
                    final[s, r] = new
                    prod[s, r] = new * pool[lax.rem(s, owned), EDGE:EDGE + planes, column(r)]
                else:
                    pot[(k + 1) % 2, r + 1, pl.ds(first, size)] = jnp.where(in_box, new, 0.0)
                return inner

            lax.fori_loop(0, tiles, one_tile, 0, unroll=4)
        return carry

    lax.fori_loop(0, slots, one_slot, 0)

    backs = [mover(-dy, -dz, live, planes) for left, right, live, dy, dz in facts]

    def terms(r, carry):
        total = [jnp.zeros((planes, LANES), jnp.float32) for o in range(3 * owned)]
        for s in range(slots):
            left, right = facts[s][:2]
            total[left] = total[left] + final[s, r] * moved[s, r]
            term = backs[s](lambda t: prod[s, t], r)
            for o in range(left + 1, min(left + 1 + REACH, 3 * owned)):
                total[o] = total[o] + jnp.where(right == o, term, 0.0)
        for o in range(3 * owned):
            seg[o, :, column(r)] = total[o]
        return carry

    lax.fori_loop(0, tiles, terms, 0, unroll=2)


def return_kernel(
    wides, seg, out, own, two, from_pair, from_two,
    local_sem, send_one, recv_one, send_two, recv_two,
):
    owned, planes, flat = out.shape
    chunk_width = flat // CHUNKS
    w = lax.axis_index("wide")
    odd = lax.rem(w, 2)
    is_odd = odd == 1
    is_even = odd == 0
    pair = w + 1 - 2 * odd
    has_two = w + 2 < wides
    takes_two = w >= 2
    sends_pair = jnp.logical_or(is_even, w + 1 < wides)
    takes_pair = jnp.logical_or(is_odd, has_two)
    even_two = jnp.logical_and(is_even, has_two)

    own_copy = pltpu.make_async_copy(seg.at[pl.ds(0, owned)], own, local_sem.at[0])
    two_copy = pltpu.make_async_copy(seg.at[pl.ds(2 * owned, owned)], two, local_sem.at[1])
    own_copy.start()
    two_copy.start()
    enter([
        (w >= 0, {"wide": pair}), (takes_two, {"wide": w - 2}), (has_two, {"wide": w + 2}),
    ])

    def columns(c):
        return pl.ds(c * chunk_width, chunk_width)

    def back_to_pair(c):
        return remote(
            seg.at[pl.ds(owned, owned), :, columns(c)], from_pair.at[:, :, columns(c)],
            send_one.at[c], recv_one.at[c], {"wide": pair},
        )

    def back_to_two(c):
        return remote(
            two.at[:, :, columns(c)], from_two.at[:, :, columns(c)],
            send_two.at[c], recv_two.at[c], {"wide": w + 2},
        )

    for c in range(CHUNKS):
        @pl.when(sends_pair)
        def _(c=c):
            back_to_pair(c).start()
    two_copy.wait()
    for c in range(CHUNKS):
        @pl.when(jnp.logical_and(is_odd, has_two))
        def _(c=c):
            back_to_two(c).start()
    for c in range(CHUNKS):
        @pl.when(takes_pair)
        def _(c=c):
            back_to_pair(c).wait_recv()

        @pl.when(even_two)
        def _(c=c):
            two[:, :, columns(c)] += from_pair[:, :, columns(c)]
            back_to_two(c).start()
    own_copy.wait()
    for c in range(CHUNKS):
        out[:, :, columns(c)] = own[:, :, columns(c)]

        @pl.when(is_odd)
        def _(c=c):
            out[:, :, columns(c)] += from_pair[:, :, columns(c)]

        @pl.when(takes_two)
        def _(c=c):
            back_to_two(c).wait_recv()
            out[:, :, columns(c)] += from_two[:, :, columns(c)]
    for c in range(CHUNKS):
        @pl.when(sends_pair)
        def _(c=c):
            back_to_pair(c).wait_send()

        @pl.when(has_two)
        def _(c=c):
            back_to_two(c).wait_send()


def per_device(wides, quads, orbitals, corners, pair_partner, pair_live):
    owned, planes, flat = orbitals.shape
    slots = pair_partner.shape[0]
    tiles = flat // LANES
    field_rows = planes + 2 * LOW
    corner_block = jnp.zeros((8, LANES), jnp.int32).at[:owned, :2].set(corners)
    f32 = jnp.float32
    dma = pltpu.SemaphoreType.DMA
    vmem = pl.BlockSpec(memory_space=pltpu.VMEM)
    smem = pl.BlockSpec(memory_space=pltpu.SMEM)
    anywhere = pl.BlockSpec(memory_space=pl.ANY)
    limit = 32 * 1024 * 1024
    pool, pool_corner = pl.pallas_call(
        functools.partial(gather_kernel, wides, quads),
        out_shape=(
            jax.ShapeDtypeStruct((3 * owned, planes + 2 * EDGE, flat), f32),
            jax.ShapeDtypeStruct((3, 8, LANES), jnp.int32),
        ),
        in_specs=[anywhere, anywhere],
        out_specs=(anywhere, anywhere),
        scratch_shapes=[
            dma((2,)), dma((2,)), dma((2,)),
            dma((CHUNKS,)), dma((CHUNKS,)), dma((CHUNKS,)), dma((CHUNKS,)),
            dma((2, 2, CHUNKS)), dma((2, 2, CHUNKS)), dma((2,)), dma((2,)),
        ],
        compiler_params=pltpu.CompilerParams(
            collective_id=0, has_side_effects=True, vmem_limit_bytes=limit
        ),
        name="gather",
    )(orbitals, corner_block)
    seg = pl.pallas_call(
        functools.partial(exchange_kernel, quads),
        out_shape=jax.ShapeDtypeStruct((3 * owned, planes, flat), f32),
        in_specs=[vmem, smem, smem, smem],
        out_specs=vmem,
        scratch_shapes=[
            pltpu.VMEM((slots, tiles + 2, field_rows, LANES), f32),
            pltpu.VMEM((slots, tiles, planes, LANES), f32),
            pltpu.VMEM((2, tiles + 2, field_rows, LANES), f32),
            pltpu.VMEM((slots, tiles, planes, LANES), f32),
            pltpu.VMEM((slots, tiles, planes, LANES), f32),
        ],
        compiler_params=pltpu.CompilerParams(vmem_limit_bytes=limit),
        name="exchange",
    )(pool, pool_corner, pair_partner, pair_live)
    return pl.pallas_call(
        functools.partial(return_kernel, wides),
        out_shape=jax.ShapeDtypeStruct(orbitals.shape, f32),
        in_specs=[anywhere],
        out_specs=vmem,
        scratch_shapes=[
            pltpu.VMEM((owned, planes, flat), f32),
            pltpu.VMEM((owned, planes, flat), f32),
            pltpu.VMEM((owned, planes, flat), f32),
            pltpu.VMEM((owned, planes, flat), f32),
            dma((2,)), dma((CHUNKS,)), dma((CHUNKS,)), dma((CHUNKS,)), dma((CHUNKS,)),
        ],
        compiler_params=pltpu.CompilerParams(
            collective_id=1, has_side_effects=True, vmem_limit_bytes=limit
        ),
        name="give_back",
    )(seg)


def solution(mesh):
    in_specs = (P("wide", "quad", None), P("wide", None), P("wide"), P("wide"))
    out_specs = P("wide", "quad", None)
    body = functools.partial(per_device, mesh.shape["wide"], mesh.shape["quad"])
    return jax.shard_map(
        body, mesh=mesh, in_specs=in_specs, out_specs=out_specs, check_vma=False
    )
```

```python
import functools
import math

import jax
import jax.numpy as jnp
from jax import lax
from jax.experimental import pallas as pl
from jax.experimental.pallas import tpu as pltpu
from jax.sharding import PartitionSpec as P

BZ = 64
SPAN = 16
SWEEPS = 8
REACH = 4
LANES = 128
EDGE = 8
LOW = 16
CHUNKS = 8
AHEAD = 3
GROUP = 4
MESH = pl.DeviceIdType.MESH


def sweep_weights():
    low = 0.5 / 6.5
    high = 12.5 / 6.5
    center = (high + low) / 2.0
    half = (high - low) / 2.0
    return [
        1.0 / (center + half * math.cos(math.pi * (2 * k + 1) / (2 * SWEEPS)))
        for k in range(SWEEPS)
    ]


def remote(src, dst, send, recv, target):
    return pltpu.make_async_remote_copy(
        src_ref=src, dst_ref=dst, send_sem=send, recv_sem=recv,
        device_id=target, device_id_type=MESH,
    )


def enter(near):
    barrier = pltpu.get_barrier_semaphore()
    for there, target in near:
        @pl.when(there)
        def _(target=target):
            pl.semaphore_signal(barrier, inc=1, device_id=target, device_id_type=MESH)
    count = jnp.int32(0)
    for there, target in near:
        count = count + jnp.where(there, 1, 0)
    pl.semaphore_wait(barrier, count)


def gather_kernel(
    wides, quads, orb, corner_in, pool, corner,
    local_sem, corner_send, corner_recv, send_two, recv_two, send_one, recv_one,
    edge_send, edge_recv, own_send, own_recv,
):
    owned, planes, flat = orb.shape
    chunk_width = flat // CHUNKS
    w = lax.axis_index("wide")
    q = lax.axis_index("quad")
    odd = lax.rem(w, 2)
    is_odd = odd == 1
    is_even = odd == 0
    pair = w + 1 - 2 * odd
    has_one = jnp.logical_or(is_even, w + 1 < wides)
    has_two = w + 2 < wides
    gives_two = w >= 2
    below = q >= 1
    above = q + 1 < quads
    enter([
        (w >= 1, {"wide": w - 1}), (gives_two, {"wide": w - 2}),
        (w + 1 < wides, {"wide": w + 1}), (has_two, {"wide": w + 2}),
        (below, {"quad": q - 1}), (above, {"quad": q + 1}),
    ])

    def columns(c):
        return pl.ds(c * chunk_width, chunk_width)

    def held(step, c):
        return pool.at[pl.ds(step * owned, owned), pl.ds(EDGE, planes), columns(c)]

    def corner_copy(step):
        return remote(
            corner_in, corner.at[step], corner_send.at[step - 1], corner_recv.at[step - 1],
            {"wide": w - step},
        )

    def own_to_two(c):
        return remote(
            orb.at[:, :, columns(c)], held(2, c), send_two.at[c], recv_two.at[c],
            {"wide": w - 2},
        )

    def own_to_pair(c):
        return remote(
            orb.at[:, :, columns(c)], held(1, c), send_one.at[c], recv_one.at[c],
            {"wide": pair},
        )

    def two_to_pair(c):
        return remote(held(2, c), held(1, c), send_one.at[c], recv_one.at[c], {"wide": pair})

    def own_edge(up):
        if up:
            return remote(
                orb.at[:, pl.ds(planes - EDGE, EDGE)],
                pool.at[pl.ds(0, owned), pl.ds(0, EDGE)],
                own_send.at[1], own_recv.at[1], {"quad": q + 1},
            )
        return remote(
            orb.at[:, pl.ds(0, EDGE)],
            pool.at[pl.ds(0, owned), pl.ds(EDGE + planes, EDGE)],
            own_send.at[0], own_recv.at[0], {"quad": q - 1},
        )

    def edge(step, up, c):
        rows = pl.ds(step * owned, owned)
        if up:
            src, dst, to = planes, 0, q + 1
        else:
            src, dst, to = EDGE, EDGE + planes, q - 1
        return remote(
            pool.at[rows, pl.ds(src, EDGE), columns(c)],
            pool.at[rows, pl.ds(dst, EDGE), columns(c)],
            edge_send.at[step - 1, int(up), c], edge_recv.at[step - 1, int(up), c],
            {"quad": to},
        )

    own_copy = pltpu.make_async_copy(
        orb, pool.at[pl.ds(0, owned), pl.ds(EDGE, planes)], local_sem.at[0]
    )
    corner_copy_own = pltpu.make_async_copy(corner_in, corner.at[0], local_sem.at[1])
    for step in (1, 2):
        @pl.when(w >= step)
        def _(step=step):
            corner_copy(step).start()
    paced = jnp.logical_and(is_even, has_two)
    for c in range(CHUNKS):
        @pl.when(gives_two if c < AHEAD else jnp.logical_and(gives_two, jnp.logical_not(paced)))
        def _(c=c):
            own_to_two(c).start()

        @pl.when(is_odd)
        def _(c=c):
            own_to_pair(c).start()
    own_copy.start()
    corner_copy_own.start()

    def pass_edges(step, c):
        @pl.when(below)
        def _():
            edge(step, False, c).start()

        @pl.when(above)
        def _():
            edge(step, True, c).start()

    for c in range(CHUNKS):
        @pl.when(has_two)
        def _(c=c):
            own_to_two(c).wait_recv()

            @pl.when(is_even)
            def _():
                two_to_pair(c).start()
            if c + AHEAD < CHUNKS:
                @pl.when(jnp.logical_and(is_even, gives_two))
                def _():
                    own_to_two(c + AHEAD).start()
            pass_edges(2, c)

        @pl.when(has_one)
        def _(c=c):
            own_to_pair(c).wait_recv()
            pass_edges(1, c)

        if c == 0:
            @pl.when(below)
            def _():
                own_edge(False).start()

            @pl.when(above)
            def _():
                own_edge(True).start()

    for up, takes, gives in ((False, above, below), (True, below, above)):
        @pl.when(takes)
        def _(up=up):
            own_edge(up).wait_recv()

        @pl.when(gives)
        def _(up=up):
            own_edge(up).wait_send()
        for step, have in ((2, has_two), (1, has_one)):
            for c in range(CHUNKS):
                @pl.when(jnp.logical_and(takes, have))
                def _(up=up, step=step, c=c):
                    edge(step, up, c).wait_recv()

                @pl.when(jnp.logical_and(gives, have))
                def _(up=up, step=step, c=c):
                    edge(step, up, c).wait_send()
    for step in (1, 2):
        @pl.when(w + step < wides)
        def _(step=step):
            corner_copy(step).wait_recv()

        @pl.when(w >= step)
        def _(step=step):
            corner_copy(step).wait_send()
    for c in range(CHUNKS):
        @pl.when(gives_two)
        def _(c=c):
            own_to_two(c).wait_send()

        @pl.when(jnp.logical_or(is_odd, has_two))
        def _(c=c):
            own_to_pair(c).wait_send()
    own_copy.wait()
    corner_copy_own.wait()


def exchange_kernel(
    quads, pool, corner_s, partner_ref, live_ref, seg, dens, moved, pot_a, pot_b, final, prod,
):
    total_orbs, wide_rows, flat = pool.shape
    owned = total_orbs // 3
    planes = wide_rows - 2 * EDGE
    slots = partner_ref.shape[0]
    tiles = flat // LANES
    rows_y = flat // BZ
    w = lax.axis_index("wide")
    q = lax.axis_index("quad")

    zero_rows = jnp.zeros((dens.shape[2], LANES), jnp.float32)
    for s in range(slots):
        dens[s, 0] = zero_rows
        dens[s, tiles + 1] = zero_rows
    pots = (pot_a, pot_b)
    for pot in pots:
        pot[0] = zero_rows
        pot[tiles + 1] = zero_rows

    lane = lax.broadcasted_iota(jnp.int32, (wide_rows, LANES), 1)
    zpos = lax.rem(lane, BZ)
    ylow = lane // BZ
    plane = lax.broadcasted_iota(jnp.int32, (wide_rows, LANES), 0) + (q * planes - EDGE)
    in_box = (plane >= 0) & (plane < quads * planes)

    def slot_facts(s):
        left = s % owned
        right = jnp.clip(partner_ref[s] - w * owned, 0, 3 * owned - 1)
        live = live_ref[s] != 0
        who, which = right // owned, lax.rem(right, owned)
        dy = corner_s[who, which, 0] - corner_s[0, left, 0]
        dz = corner_s[who, which, 1] - corner_s[0, left, 1]
        dy = jnp.clip(jnp.where(live, dy, 0), -SPAN, SPAN)
        dz = jnp.clip(jnp.where(live, dz, 0), -SPAN, SPAN)
        return left, right, live, dy, dz

    def mover(dy, dz, ok, rows):
        by = dy * BZ + dz
        whole = by >> 7
        rest = by & (LANES - 1)
        near_part = lane[:rows] < LANES - rest
        zfrom = zpos[:rows] - dz
        keep_z = (zfrom >= 0) & (zfrom < BZ) & ok
        yfrom = ylow[:rows] - dy

        def move(load, r):
            here = load(jnp.clip(r - whole, 0, tiles - 1))
            before = load(jnp.clip(r - whole - 1, 0, tiles - 1))
            turned = pltpu.roll(jnp.where(near_part, here, before), rest, 1)
            source = yfrom + 2 * r
            keep = keep_z & (source >= 0) & (source < rows_y)
            return jnp.where(keep, turned, 0.0)

        return move

    def column(t):
        return pl.ds(pl.multiple_of(t * LANES, LANES), LANES)

    facts = [slot_facts(s) for s in range(slots)]
    for s in range(slots):
        left, right, live, dy, dz = facts[s]
        move = mover(dy, dz, live, wide_rows)

        def one_tile(r, carry, s=s, left=left, right=right, move=move):
            there = move(lambda t: pool[right, :, column(t)], r)
            moved[s, r] = there[EDGE:EDGE + planes]
            dens[s, r + 1, LOW - EDGE:LOW + planes + EDGE] = jnp.where(
                in_box, there * pool[left, :, column(r)], 0.0
            )
            return carry

        lax.fori_loop(0, tiles, one_tile, 0, unroll=2)

    weights = sweep_weights()

    def stencil(v, before, after, up, down):
        size = v.shape[0]
        cross = v + jnp.where(lane[:size] >= BZ, before, after)
        total = (up + down) + pltpu.roll(cross, BZ, 1)
        total = total + jnp.where(zpos[:size] > 0, pltpu.roll(v, 1, 1), 0.0)
        return total + jnp.where(zpos[:size] < BZ - 1, pltpu.roll(v, LANES - 1, 1), 0.0)

    def one_slot(s, carry):
        for k in range(1, SWEEPS):
            gain = weights[k] / 6.5
            if k == 1:
                read = lambda t, first, size: dens[s, t, pl.ds(first, size)]
            else:
                read = lambda t, first, size, k=k: pots[k % 2][t, pl.ds(first, size)]
            last = k == SWEEPS - 1

            def some_tiles(i, inner, k=k, gain=gain, read=read, last=last):
                r = i * GROUP
                first, size = (LOW, planes) if last else (LOW - EDGE, wide_rows)
                here = [read(r + g, first, size) for g in range(GROUP + 2)]
                up = [read(r + g + 1, first + 1, size) for g in range(GROUP)]
                down = [read(r + g + 1, first - 1, size) for g in range(GROUP)]
                news = []
                for g in range(GROUP):
                    v = here[g + 1]
                    total = stencil(v, here[g], here[g + 2], up[g], down[g])
                    if k == 1:
                        start = weights[0] / 6.5
                        new = ((1.0 - weights[1]) * start + gain) * v + (gain * start) * total
                    else:
                        d = dens[s, r + g + 1, pl.ds(first, size)]
                        new = (1.0 - weights[k]) * v + gain * (d + total)
                    if not last:
                        new = jnp.where(in_box, new, 0.0)
                    news.append(new)
                for g in range(GROUP):
                    if last:
                        final[s, r + g] = news[g]
                        own = pool[lax.rem(s, owned), EDGE:EDGE + planes, column(r + g)]
                        prod[s, r + g] = news[g] * own
                    else:
                        pots[(k + 1) % 2][r + g + 1, pl.ds(first, size)] = news[g]
                return inner

            lax.fori_loop(0, tiles // GROUP, some_tiles, 0)
        return carry

    lax.fori_loop(0, slots, one_slot, 0)

    backs = [mover(-dy, -dz, live, planes) for left, right, live, dy, dz in facts]

    def terms(r, carry):
        total = [jnp.zeros((planes, LANES), jnp.float32) for o in range(3 * owned)]
        for s in range(slots):
            left, right = facts[s][:2]
            total[left] = total[left] + final[s, r] * moved[s, r]
            term = backs[s](lambda t: prod[s, t], r)
            for o in range(left + 1, min(left + 1 + REACH, 3 * owned)):
                total[o] = total[o] + jnp.where(right == o, term, 0.0)
        for o in range(3 * owned):
            seg[o, :, column(r)] = total[o]
        return carry

    lax.fori_loop(0, tiles, terms, 0, unroll=2)


def return_kernel(
    wides, seg, out, own, two, from_pair, from_two,
    local_sem, send_one, recv_one, send_two, recv_two,
):
    owned, planes, flat = out.shape
    chunk_width = flat // CHUNKS
    w = lax.axis_index("wide")
    odd = lax.rem(w, 2)
    is_odd = odd == 1
    is_even = odd == 0
    pair = w + 1 - 2 * odd
    has_two = w + 2 < wides
    takes_two = w >= 2
    sends_pair = jnp.logical_or(is_even, w + 1 < wides)
    takes_pair = jnp.logical_or(is_odd, has_two)
    even_two = jnp.logical_and(is_even, has_two)

    own_copy = pltpu.make_async_copy(seg.at[pl.ds(0, owned)], own, local_sem.at[0])
    two_copy = pltpu.make_async_copy(seg.at[pl.ds(2 * owned, owned)], two, local_sem.at[1])
    own_copy.start()
    two_copy.start()
    enter([
        (w >= 0, {"wide": pair}), (takes_two, {"wide": w - 2}), (has_two, {"wide": w + 2}),
    ])

    def columns(c):
        return pl.ds(c * chunk_width, chunk_width)

    def back_to_pair(c):
        return remote(
            seg.at[pl.ds(owned, owned), :, columns(c)], from_pair.at[:, :, columns(c)],
            send_one.at[c], recv_one.at[c], {"wide": pair},
        )

    def back_to_two(c):
        return remote(
            two.at[:, :, columns(c)], from_two.at[:, :, columns(c)],
            send_two.at[c], recv_two.at[c], {"wide": w + 2},
        )

    two_copy.wait()
    for c in range(CHUNKS):
        @pl.when(jnp.logical_and(sends_pair, jnp.logical_not(even_two)))
        def _(c=c):
            back_to_pair(c).start()

        @pl.when(jnp.logical_and(is_odd, has_two))
        def _(c=c):
            back_to_two(c).start()
    for c in range(CHUNKS):
        @pl.when(takes_pair)
        def _(c=c):
            back_to_pair(c).wait_recv()

        @pl.when(even_two)
        def _(c=c):
            two[:, :, columns(c)] += from_pair[:, :, columns(c)]
            back_to_two(c).start()
            back_to_pair(c).start()
    own_copy.wait()
    for c in range(CHUNKS):
        out[:, :, columns(c)] = own[:, :, columns(c)]

        @pl.when(is_odd)
        def _(c=c):
            out[:, :, columns(c)] += from_pair[:, :, columns(c)]

        @pl.when(takes_two)
        def _(c=c):
            back_to_two(c).wait_recv()
            out[:, :, columns(c)] += from_two[:, :, columns(c)]
    for c in range(CHUNKS):
        @pl.when(sends_pair)
        def _(c=c):
            back_to_pair(c).wait_send()

        @pl.when(has_two)
        def _(c=c):
            back_to_two(c).wait_send()


def per_device(wides, quads, orbitals, corners, pair_partner, pair_live):
    owned, planes, flat = orbitals.shape
    slots = pair_partner.shape[0]
    tiles = flat // LANES
    field_rows = planes + 2 * LOW
    corner_block = jnp.zeros((8, LANES), jnp.int32).at[:owned, :2].set(corners)
    f32 = jnp.float32
    dma = pltpu.SemaphoreType.DMA
    vmem = pl.BlockSpec(memory_space=pltpu.VMEM)
    smem = pl.BlockSpec(memory_space=pltpu.SMEM)
    anywhere = pl.BlockSpec(memory_space=pl.ANY)
    limit = 32 * 1024 * 1024
    pool, pool_corner = pl.pallas_call(
        functools.partial(gather_kernel, wides, quads),
        out_shape=(
            jax.ShapeDtypeStruct((3 * owned, planes + 2 * EDGE, flat), f32),
            jax.ShapeDtypeStruct((3, 8, LANES), jnp.int32),
        ),
        in_specs=[anywhere, anywhere],
        out_specs=(anywhere, anywhere),
        scratch_shapes=[
            dma((2,)), dma((2,)), dma((2,)),
            dma((CHUNKS,)), dma((CHUNKS,)), dma((CHUNKS,)), dma((CHUNKS,)),
            dma((2, 2, CHUNKS)), dma((2, 2, CHUNKS)), dma((2,)), dma((2,)),
        ],
        compiler_params=pltpu.CompilerParams(
            collective_id=0, has_side_effects=True, vmem_limit_bytes=limit
        ),
        name="gather",
    )(orbitals, corner_block)
    seg = pl.pallas_call(
        functools.partial(exchange_kernel, quads),
        out_shape=jax.ShapeDtypeStruct((3 * owned, planes, flat), f32),
        in_specs=[vmem, smem, smem, smem],
        out_specs=vmem,
        scratch_shapes=[
            pltpu.VMEM((slots, tiles + 2, field_rows, LANES), f32),
            pltpu.VMEM((slots, tiles, planes, LANES), f32),
            pltpu.VMEM((tiles + 2, field_rows, LANES), f32),
            pltpu.VMEM((tiles + 2, field_rows, LANES), f32),
            pltpu.VMEM((slots, tiles, planes, LANES), f32),
            pltpu.VMEM((slots, tiles, planes, LANES), f32),
        ],
        compiler_params=pltpu.CompilerParams(vmem_limit_bytes=limit),
        name="exchange",
    )(pool, pool_corner, pair_partner, pair_live)
    return pl.pallas_call(
        functools.partial(return_kernel, wides),
        out_shape=jax.ShapeDtypeStruct(orbitals.shape, f32),
        in_specs=[anywhere],
        out_specs=vmem,
        scratch_shapes=[
            pltpu.VMEM((owned, planes, flat), f32),
            pltpu.VMEM((owned, planes, flat), f32),
            pltpu.VMEM((owned, planes, flat), f32),
            pltpu.VMEM((owned, planes, flat), f32),
            dma((2,)), dma((CHUNKS,)), dma((CHUNKS,)), dma((CHUNKS,)), dma((CHUNKS,)),
        ],
        compiler_params=pltpu.CompilerParams(
            collective_id=1, has_side_effects=True, vmem_limit_bytes=limit
        ),
        name="give_back",
    )(seg)


def solution(mesh):
    in_specs = (P("wide", "quad", None), P("wide", None), P("wide"), P("wide"))
    out_specs = P("wide", "quad", None)
    body = functools.partial(per_device, mesh.shape["wide"], mesh.shape["quad"])
    return jax.shard_map(
        body, mesh=mesh, in_specs=in_specs, out_specs=out_specs, check_vma=False
    )
```

```python
import functools
import math

import jax
import jax.numpy as jnp
import numpy as np
from jax import lax
from jax.experimental import pallas as pl
from jax.experimental.pallas import tpu as pltpu
from jax.sharding import PartitionSpec as P

BZ = 64
SPAN = 16
SWEEPS = 8
REACH = 4
LANES = 128
EDGE = 8
LOW = 16
CHUNKS = 8
AHEAD = 3
GROUP = 4
MESH = pl.DeviceIdType.MESH


def sweep_weights():
    low = 0.5 / 6.5
    high = 12.5 / 6.5
    center = (high + low) / 2.0
    half = (high - low) / 2.0
    return [
        1.0 / (center + half * math.cos(math.pi * (2 * k + 1) / (2 * SWEEPS)))
        for k in range(SWEEPS)
    ]


def sine_table():
    count = np.arange(1, BZ + 1)
    sine = np.sqrt(2.0 / (BZ + 1)) * np.sin(np.pi * np.outer(count, count) / (BZ + 1))
    both = np.kron(np.eye(LANES // BZ), sine)
    factor = np.tile(2.0 * np.cos(np.pi * count / (BZ + 1)), LANES // BZ)
    return np.concatenate([both, np.tile(factor, (8, 1))]).astype(np.float32)


def remote(src, dst, send, recv, target):
    return pltpu.make_async_remote_copy(
        src_ref=src, dst_ref=dst, send_sem=send, recv_sem=recv,
        device_id=target, device_id_type=MESH,
    )


def enter(near):
    barrier = pltpu.get_barrier_semaphore()
    for there, target in near:
        @pl.when(there)
        def _(target=target):
            pl.semaphore_signal(barrier, inc=1, device_id=target, device_id_type=MESH)
    count = jnp.int32(0)
    for there, target in near:
        count = count + jnp.where(there, 1, 0)
    pl.semaphore_wait(barrier, count)


def gather_kernel(
    wides, quads, orb, corner_in, pool, corner,
    local_sem, corner_send, corner_recv, send_two, recv_two, send_one, recv_one,
    edge_send, edge_recv, own_send, own_recv,
):
    owned, planes, flat = orb.shape
    chunk_width = flat // CHUNKS
    w = lax.axis_index("wide")
    q = lax.axis_index("quad")
    odd = lax.rem(w, 2)
    is_odd = odd == 1
    is_even = odd == 0
    pair = w + 1 - 2 * odd
    has_one = jnp.logical_or(is_even, w + 1 < wides)
    has_two = w + 2 < wides
    gives_two = w >= 2
    below = q >= 1
    above = q + 1 < quads
    enter([
        (w >= 1, {"wide": w - 1}), (gives_two, {"wide": w - 2}),
        (w + 1 < wides, {"wide": w + 1}), (has_two, {"wide": w + 2}),
        (below, {"quad": q - 1}), (above, {"quad": q + 1}),
    ])

    def columns(c):
        return pl.ds(c * chunk_width, chunk_width)

    def held(step, c):
        return pool.at[pl.ds(step * owned, owned), pl.ds(EDGE, planes), columns(c)]

    def corner_copy(step):
        return remote(
            corner_in, corner.at[step], corner_send.at[step - 1], corner_recv.at[step - 1],
            {"wide": w - step},
        )

    def own_to_two(c):
        return remote(
            orb.at[:, :, columns(c)], held(2, c), send_two.at[c], recv_two.at[c],
            {"wide": w - 2},
        )

    def own_to_pair(c):
        return remote(
            orb.at[:, :, columns(c)], held(1, c), send_one.at[c], recv_one.at[c],
            {"wide": pair},
        )

    def two_to_pair(c):
        return remote(held(2, c), held(1, c), send_one.at[c], recv_one.at[c], {"wide": pair})

    def own_edge(up):
        if up:
            return remote(
                orb.at[:, pl.ds(planes - EDGE, EDGE)],
                pool.at[pl.ds(0, owned), pl.ds(0, EDGE)],
                own_send.at[1], own_recv.at[1], {"quad": q + 1},
            )
        return remote(
            orb.at[:, pl.ds(0, EDGE)],
            pool.at[pl.ds(0, owned), pl.ds(EDGE + planes, EDGE)],
            own_send.at[0], own_recv.at[0], {"quad": q - 1},
        )

    def edge(step, up, c):
        rows = pl.ds(step * owned, owned)
        if up:
            src, dst, to = planes, 0, q + 1
        else:
            src, dst, to = EDGE, EDGE + planes, q - 1
        return remote(
            pool.at[rows, pl.ds(src, EDGE), columns(c)],
            pool.at[rows, pl.ds(dst, EDGE), columns(c)],
            edge_send.at[step - 1, int(up), c], edge_recv.at[step - 1, int(up), c],
            {"quad": to},
        )

    own_copy = pltpu.make_async_copy(
        orb, pool.at[pl.ds(0, owned), pl.ds(EDGE, planes)], local_sem.at[0]
    )
    corner_copy_own = pltpu.make_async_copy(corner_in, corner.at[0], local_sem.at[1])
    for step in (1, 2):
        @pl.when(w >= step)
        def _(step=step):
            corner_copy(step).start()
    paced = jnp.logical_and(is_even, has_two)
    for c in range(CHUNKS):
        @pl.when(gives_two if c < AHEAD else jnp.logical_and(gives_two, jnp.logical_not(paced)))
        def _(c=c):
            own_to_two(c).start()

        @pl.when(is_odd)
        def _(c=c):
            own_to_pair(c).start()
    own_copy.start()
    corner_copy_own.start()

    def pass_edges(step, c):
        @pl.when(below)
        def _():
            edge(step, False, c).start()

        @pl.when(above)
        def _():
            edge(step, True, c).start()

    for c in range(CHUNKS):
        @pl.when(has_two)
        def _(c=c):
            own_to_two(c).wait_recv()

            @pl.when(is_even)
            def _():
                two_to_pair(c).start()
            if c + AHEAD < CHUNKS:
                @pl.when(jnp.logical_and(is_even, gives_two))
                def _():
                    own_to_two(c + AHEAD).start()
            pass_edges(2, c)

        @pl.when(has_one)
        def _(c=c):
            own_to_pair(c).wait_recv()
            pass_edges(1, c)

        if c == 0:
            @pl.when(below)
            def _():
                own_edge(False).start()

            @pl.when(above)
            def _():
                own_edge(True).start()

    for up, takes, gives in ((False, above, below), (True, below, above)):
        @pl.when(takes)
        def _(up=up):
            own_edge(up).wait_recv()

        @pl.when(gives)
        def _(up=up):
            own_edge(up).wait_send()
        for step, have in ((2, has_two), (1, has_one)):
            for c in range(CHUNKS):
                @pl.when(jnp.logical_and(takes, have))
                def _(up=up, step=step, c=c):
                    edge(step, up, c).wait_recv()

                @pl.when(jnp.logical_and(gives, have))
                def _(up=up, step=step, c=c):
                    edge(step, up, c).wait_send()
    for step in (1, 2):
        @pl.when(w + step < wides)
        def _(step=step):
            corner_copy(step).wait_recv()

        @pl.when(w >= step)
        def _(step=step):
            corner_copy(step).wait_send()
    for c in range(CHUNKS):
        @pl.when(gives_two)
        def _(c=c):
            own_to_two(c).wait_send()

        @pl.when(jnp.logical_or(is_odd, has_two))
        def _(c=c):
            own_to_pair(c).wait_send()
    own_copy.wait()
    corner_copy_own.wait()


def exchange_kernel(
    quads, pool, corner_s, partner_ref, live_ref, table, seg, dens, moved, pot_a, pot_b, final, prod,
):
    total_orbs, wide_rows, flat = pool.shape
    owned = total_orbs // 3
    planes = wide_rows - 2 * EDGE
    slots = partner_ref.shape[0]
    tiles = flat // LANES
    rows_y = flat // BZ
    w = lax.axis_index("wide")
    q = lax.axis_index("quad")

    lane = lax.broadcasted_iota(jnp.int32, (wide_rows, LANES), 1)
    zpos = lax.rem(lane, BZ)
    ylow = lane // BZ
    plane = lax.broadcasted_iota(jnp.int32, (wide_rows, LANES), 0) + (q * planes - EDGE)
    in_box = (plane >= 0) & (plane < quads * planes)

    def slot_facts(s):
        left = s % owned
        right = jnp.clip(partner_ref[s] - w * owned, 0, 3 * owned - 1)
        live = live_ref[s] != 0
        who, which = right // owned, lax.rem(right, owned)
        dy = corner_s[who, which, 0] - corner_s[0, left, 0]
        dz = corner_s[who, which, 1] - corner_s[0, left, 1]
        dy = jnp.clip(jnp.where(live, dy, 0), -SPAN, SPAN)
        dz = jnp.clip(jnp.where(live, dz, 0), -SPAN, SPAN)
        return left, right, live, dy, dz

    def mover(dy, dz, ok, rows):
        by = dy * BZ + dz
        whole = by >> 7
        rest = by & (LANES - 1)
        near_part = lane[:rows] < LANES - rest
        zfrom = zpos[:rows] - dz
        keep_z = (zfrom >= 0) & (zfrom < BZ) & ok
        yfrom = ylow[:rows] - dy

        def move(load, r):
            here = load(jnp.clip(r - whole, 0, tiles - 1))
            before = load(jnp.clip(r - whole - 1, 0, tiles - 1))
            turned = pltpu.roll(jnp.where(near_part, here, before), rest, 1)
            source = yfrom + 2 * r
            keep = keep_z & (source >= 0) & (source < rows_y)
            return jnp.where(keep, turned, 0.0)

        return move

    def column(t):
        return pl.ds(pl.multiple_of(t * LANES, LANES), LANES)

    half = tiles // 2
    factor = table[LANES:LANES + 8]

    def transform(rows):
        return jnp.dot(
            rows, table[0:LANES], precision=lax.Precision.HIGHEST,
            preferred_element_type=jnp.float32,
        )

    def regroup(a, b):
        low = lane[:a.shape[0]] < BZ
        return (
            jnp.where(low, a, pltpu.roll(b, BZ, 1)), jnp.where(low, pltpu.roll(a, BZ, 1), b)
        )

    def guard(field):
        rows = pl.ds(LOW - EDGE, wide_rows)
        field[0, rows] = jnp.where(lane >= BZ, pltpu.roll(field[tiles, rows], BZ, 1), 0.0)
        field[tiles + 1, rows] = jnp.where(lane < BZ, pltpu.roll(field[1, rows], BZ, 1), 0.0)

    facts = [slot_facts(s) for s in range(slots)]
    for s in range(slots):
        left, right, live, dy, dz = facts[s]
        move = mover(dy, dz, live, wide_rows)

        def two_tiles(i, carry, s=s, left=left, right=right, move=move):
            parts = []
            for r in (i, i + half):
                there = move(lambda t: pool[right, :, column(t)], r)
                moved[s, r] = there[EDGE:EDGE + planes]
                parts.append(jnp.where(in_box, there * pool[left, :, column(r)], 0.0))
            waves = transform(jnp.concatenate(regroup(*parts)))
            dens[s, 2 * i + 1, LOW - EDGE:LOW + planes + EDGE] = waves[:wide_rows]
            dens[s, 2 * i + 2, LOW - EDGE:LOW + planes + EDGE] = waves[wide_rows:]
            return carry

        lax.fori_loop(0, half, two_tiles, 0, unroll=2)
        guard(dens.at[s])

    weights = sweep_weights()
    pots = (pot_a, pot_b)

    def one_slot(s, carry):
        for k in range(1, SWEEPS):
            gain = weights[k] / 6.5
            if k == 1:
                read = lambda t, first, size: dens[s, t, pl.ds(first, size)]
            else:
                read = lambda t, first, size, k=k: pots[k % 2][t, pl.ds(first, size)]
            last = k == SWEEPS - 1

            first, size = (LOW, planes) if last else (LOW - EDGE, wide_rows)
            if k == 1:
                start = weights[0] / 6.5
                keep = (1.0 - weights[1]) * start + gain + gain * start * factor
                gain = gain * start
            else:
                keep = (1.0 - weights[k]) + gain * factor
            keep = jnp.concatenate([keep] * (size // 8))

            def some_tiles(i, inner, k=k, gain=gain, read=read, last=last, keep=keep, first=first, size=size):
                r = i * GROUP
                here = [read(r + g, first, size) for g in range(GROUP + 2)]
                news = []
                for g in range(GROUP):
                    total = read(r + g + 1, first + 1, size) + read(r + g + 1, first - 1, size)
                    total = total + (here[g] + here[g + 2])
                    if k > 1:
                        total = total + dens[s, r + g + 1, pl.ds(first, size)]
                    new = keep * here[g + 1] + gain * total
                    if not last:
                        new = jnp.where(in_box, new, 0.0)
                    news.append(new)
                if last:
                    cells = transform(jnp.concatenate(news))
                    for g in range(0, GROUP, 2):
                        t = i * (GROUP // 2) + g // 2
                        pair = regroup(
                            cells[g * planes:(g + 1) * planes],
                            cells[(g + 1) * planes:(g + 2) * planes],
                        )
                        for place, value in zip((t, t + half), pair):
                            final[s, place] = value
                            own = pool[lax.rem(s, owned), EDGE:EDGE + planes, column(place)]
                            prod[s, place] = value * own
                else:
                    for g in range(GROUP):
                        pots[(k + 1) % 2][r + g + 1, pl.ds(first, size)] = news[g]
                return inner

            lax.fori_loop(0, tiles // GROUP, some_tiles, 0)
            if not last:
                guard(pots[(k + 1) % 2])
        return carry

    lax.fori_loop(0, slots, one_slot, 0)

    backs = [mover(-dy, -dz, live, planes) for left, right, live, dy, dz in facts]

    def terms(r, carry):
        total = [jnp.zeros((planes, LANES), jnp.float32) for o in range(3 * owned)]
        for s in range(slots):
            left, right = facts[s][:2]
            total[left] = total[left] + final[s, r] * moved[s, r]
            term = backs[s](lambda t: prod[s, t], r)
            for o in range(left + 1, min(left + 1 + REACH, 3 * owned)):
                total[o] = total[o] + jnp.where(right == o, term, 0.0)
        for o in range(3 * owned):
            seg[o, :, column(r)] = total[o]
        return carry

    lax.fori_loop(0, tiles, terms, 0, unroll=2)


def return_kernel(
    wides, seg, out, own, two, from_pair, from_two,
    local_sem, send_one, recv_one, send_two, recv_two,
):
    owned, planes, flat = out.shape
    chunk_width = flat // CHUNKS
    w = lax.axis_index("wide")
    odd = lax.rem(w, 2)
    is_odd = odd == 1
    is_even = odd == 0
    pair = w + 1 - 2 * odd
    has_two = w + 2 < wides
    takes_two = w >= 2
    sends_pair = jnp.logical_or(is_even, w + 1 < wides)
    takes_pair = jnp.logical_or(is_odd, has_two)
    even_two = jnp.logical_and(is_even, has_two)

    own_copy = pltpu.make_async_copy(seg.at[pl.ds(0, owned)], own, local_sem.at[0])
    two_copy = pltpu.make_async_copy(seg.at[pl.ds(2 * owned, owned)], two, local_sem.at[1])
    own_copy.start()
    two_copy.start()
    enter([
        (w >= 0, {"wide": pair}), (takes_two, {"wide": w - 2}), (has_two, {"wide": w + 2}),
    ])

    def columns(c):
        return pl.ds(c * chunk_width, chunk_width)

    def back_to_pair(c):
        return remote(
            seg.at[pl.ds(owned, owned), :, columns(c)], from_pair.at[:, :, columns(c)],
            send_one.at[c], recv_one.at[c], {"wide": pair},
        )

    def back_to_two(c):
        return remote(
            two.at[:, :, columns(c)], from_two.at[:, :, columns(c)],
            send_two.at[c], recv_two.at[c], {"wide": w + 2},
        )

    two_copy.wait()
    for c in range(CHUNKS):
        @pl.when(jnp.logical_and(sends_pair, jnp.logical_not(even_two)))
        def _(c=c):
            back_to_pair(c).start()

        @pl.when(jnp.logical_and(is_odd, has_two))
        def _(c=c):
            back_to_two(c).start()
    for c in range(CHUNKS):
        @pl.when(takes_pair)
        def _(c=c):
            back_to_pair(c).wait_recv()

        @pl.when(even_two)
        def _(c=c):
            two[:, :, columns(c)] += from_pair[:, :, columns(c)]
            back_to_two(c).start()
            back_to_pair(c).start()
    own_copy.wait()
    for c in range(CHUNKS):
        out[:, :, columns(c)] = own[:, :, columns(c)]

        @pl.when(is_odd)
        def _(c=c):
            out[:, :, columns(c)] += from_pair[:, :, columns(c)]

        @pl.when(takes_two)
        def _(c=c):
            back_to_two(c).wait_recv()
            out[:, :, columns(c)] += from_two[:, :, columns(c)]
    for c in range(CHUNKS):
        @pl.when(sends_pair)
        def _(c=c):
            back_to_pair(c).wait_send()

        @pl.when(has_two)
        def _(c=c):
            back_to_two(c).wait_send()


def per_device(wides, quads, orbitals, corners, pair_partner, pair_live):
    owned, planes, flat = orbitals.shape
    slots = pair_partner.shape[0]
    tiles = flat // LANES
    field_rows = planes + 2 * LOW
    corner_block = jnp.zeros((8, LANES), jnp.int32).at[:owned, :2].set(corners)
    f32 = jnp.float32
    dma = pltpu.SemaphoreType.DMA
    vmem = pl.BlockSpec(memory_space=pltpu.VMEM)
    smem = pl.BlockSpec(memory_space=pltpu.SMEM)
    anywhere = pl.BlockSpec(memory_space=pl.ANY)
    limit = 32 * 1024 * 1024
    pool, pool_corner = pl.pallas_call(
        functools.partial(gather_kernel, wides, quads),
        out_shape=(
            jax.ShapeDtypeStruct((3 * owned, planes + 2 * EDGE, flat), f32),
            jax.ShapeDtypeStruct((3, 8, LANES), jnp.int32),
        ),
        in_specs=[anywhere, anywhere],
        out_specs=(anywhere, anywhere),
        scratch_shapes=[
            dma((2,)), dma((2,)), dma((2,)),
            dma((CHUNKS,)), dma((CHUNKS,)), dma((CHUNKS,)), dma((CHUNKS,)),
            dma((2, 2, CHUNKS)), dma((2, 2, CHUNKS)), dma((2,)), dma((2,)),
        ],
        compiler_params=pltpu.CompilerParams(
            collective_id=0, has_side_effects=True, vmem_limit_bytes=limit
        ),
        name="gather",
    )(orbitals, corner_block)
    seg = pl.pallas_call(
        functools.partial(exchange_kernel, quads),
        out_shape=jax.ShapeDtypeStruct((3 * owned, planes, flat), f32),
        in_specs=[vmem, smem, smem, smem, vmem],
        out_specs=vmem,
        scratch_shapes=[
            pltpu.VMEM((slots, tiles + 2, field_rows, LANES), f32),
            pltpu.VMEM((slots, tiles, planes, LANES), f32),
            pltpu.VMEM((tiles + 2, field_rows, LANES), f32),
            pltpu.VMEM((tiles + 2, field_rows, LANES), f32),
            pltpu.VMEM((slots, tiles, planes, LANES), f32),
            pltpu.VMEM((slots, tiles, planes, LANES), f32),
        ],
        compiler_params=pltpu.CompilerParams(vmem_limit_bytes=limit),
        name="exchange",
    )(pool, pool_corner, pair_partner, pair_live, jnp.asarray(sine_table()))
    return pl.pallas_call(
        functools.partial(return_kernel, wides),
        out_shape=jax.ShapeDtypeStruct(orbitals.shape, f32),
        in_specs=[anywhere],
        out_specs=vmem,
        scratch_shapes=[
            pltpu.VMEM((owned, planes, flat), f32),
            pltpu.VMEM((owned, planes, flat), f32),
            pltpu.VMEM((owned, planes, flat), f32),
            pltpu.VMEM((owned, planes, flat), f32),
            dma((2,)), dma((CHUNKS,)), dma((CHUNKS,)), dma((CHUNKS,)), dma((CHUNKS,)),
        ],
        compiler_params=pltpu.CompilerParams(
            collective_id=1, has_side_effects=True, vmem_limit_bytes=limit
        ),
        name="give_back",
    )(seg)


def solution(mesh):
    in_specs = (P("wide", "quad", None), P("wide", None), P("wide"), P("wide"))
    out_specs = P("wide", "quad", None)
    body = functools.partial(per_device, mesh.shape["wide"], mesh.shape["quad"])
    return jax.shard_map(
        body, mesh=mesh, in_specs=in_specs, out_specs=out_specs, check_vma=False
    )
```

```python
import functools
import math

import jax
import jax.numpy as jnp
import numpy as np
from jax import lax
from jax.experimental import pallas as pl
from jax.experimental.pallas import tpu as pltpu
from jax.sharding import PartitionSpec as P

BZ = 64
SPAN = 16
SWEEPS = 8
REACH = 4
LANES = 128
EDGE = 8
LOW = 16
CHUNKS = 8
AHEAD = 3
BLOCK = 8
GROUP = 4
MESH = pl.DeviceIdType.MESH


def sweep_weights():
    low = 0.5 / 6.5
    high = 12.5 / 6.5
    center = (high + low) / 2.0
    half = (high - low) / 2.0
    return [
        1.0 / (center + half * math.cos(math.pi * (2 * k + 1) / (2 * SWEEPS)))
        for k in range(SWEEPS)
    ]


def sine_table():
    count = np.arange(1, BZ + 1)
    sine = np.sqrt(2.0 / (BZ + 1)) * np.sin(np.pi * np.outer(count, count) / (BZ + 1))
    both = np.kron(np.eye(LANES // BZ), sine)
    factor = np.tile(2.0 * np.cos(np.pi * count / (BZ + 1)), LANES // BZ)
    return np.concatenate([both, np.tile(factor, (8, 1))]).astype(np.float32)


def remote(src, dst, send, recv, target):
    return pltpu.make_async_remote_copy(
        src_ref=src, dst_ref=dst, send_sem=send, recv_sem=recv,
        device_id=target, device_id_type=MESH,
    )


def enter(near):
    barrier = pltpu.get_barrier_semaphore()
    for there, target in near:
        @pl.when(there)
        def _(target=target):
            pl.semaphore_signal(barrier, inc=1, device_id=target, device_id_type=MESH)
    count = jnp.int32(0)
    for there, target in near:
        count = count + jnp.where(there, 1, 0)
    pl.semaphore_wait(barrier, count)


def gather_kernel(
    wides, quads, orb, corner_in, pool, corner,
    local_sem, corner_send, corner_recv, send_two, recv_two, send_one, recv_one,
    edge_send, edge_recv, own_send, own_recv,
):
    owned, planes, flat = orb.shape
    chunk_width = flat // CHUNKS
    w = lax.axis_index("wide")
    q = lax.axis_index("quad")
    odd = lax.rem(w, 2)
    is_odd = odd == 1
    is_even = odd == 0
    pair = w + 1 - 2 * odd
    has_one = jnp.logical_or(is_even, w + 1 < wides)
    has_two = w + 2 < wides
    gives_two = w >= 2
    below = q >= 1
    above = q + 1 < quads
    enter([
        (w >= 1, {"wide": w - 1}), (gives_two, {"wide": w - 2}),
        (w + 1 < wides, {"wide": w + 1}), (has_two, {"wide": w + 2}),
        (below, {"quad": q - 1}), (above, {"quad": q + 1}),
    ])

    def columns(c):
        return pl.ds(c * chunk_width, chunk_width)

    def held(step, c):
        return pool.at[pl.ds(step * owned, owned), pl.ds(EDGE, planes), columns(c)]

    def corner_copy(step):
        return remote(
            corner_in, corner.at[step], corner_send.at[step - 1], corner_recv.at[step - 1],
            {"wide": w - step},
        )

    def own_to_two(c):
        return remote(
            orb.at[:, :, columns(c)], held(2, c), send_two.at[c], recv_two.at[c],
            {"wide": w - 2},
        )

    def own_to_pair(c):
        return remote(
            orb.at[:, :, columns(c)], held(1, c), send_one.at[c], recv_one.at[c],
            {"wide": pair},
        )

    def two_to_pair(c):
        return remote(held(2, c), held(1, c), send_one.at[c], recv_one.at[c], {"wide": pair})

    def own_edge(up):
        if up:
            return remote(
                orb.at[:, pl.ds(planes - EDGE, EDGE)],
                pool.at[pl.ds(0, owned), pl.ds(0, EDGE)],
                own_send.at[1], own_recv.at[1], {"quad": q + 1},
            )
        return remote(
            orb.at[:, pl.ds(0, EDGE)],
            pool.at[pl.ds(0, owned), pl.ds(EDGE + planes, EDGE)],
            own_send.at[0], own_recv.at[0], {"quad": q - 1},
        )

    def edge(step, up, c):
        rows = pl.ds(step * owned, owned)
        if up:
            src, dst, to = planes, 0, q + 1
        else:
            src, dst, to = EDGE, EDGE + planes, q - 1
        return remote(
            pool.at[rows, pl.ds(src, EDGE), columns(c)],
            pool.at[rows, pl.ds(dst, EDGE), columns(c)],
            edge_send.at[step - 1, int(up), c], edge_recv.at[step - 1, int(up), c],
            {"quad": to},
        )

    own_copy = pltpu.make_async_copy(
        orb, pool.at[pl.ds(0, owned), pl.ds(EDGE, planes)], local_sem.at[0]
    )
    corner_copy_own = pltpu.make_async_copy(corner_in, corner.at[0], local_sem.at[1])
    for step in (1, 2):
        @pl.when(w >= step)
        def _(step=step):
            corner_copy(step).start()
    paced = jnp.logical_and(is_even, has_two)
    for c in range(CHUNKS):
        @pl.when(gives_two if c < AHEAD else jnp.logical_and(gives_two, jnp.logical_not(paced)))
        def _(c=c):
            own_to_two(c).start()

        @pl.when(is_odd)
        def _(c=c):
            own_to_pair(c).start()
    own_copy.start()
    corner_copy_own.start()

    def pass_edges(step, c):
        @pl.when(below)
        def _():
            edge(step, False, c).start()

        @pl.when(above)
        def _():
            edge(step, True, c).start()

    for c in range(CHUNKS):
        @pl.when(has_two)
        def _(c=c):
            own_to_two(c).wait_recv()

            @pl.when(is_even)
            def _():
                two_to_pair(c).start()
            if c + AHEAD < CHUNKS:
                @pl.when(jnp.logical_and(is_even, gives_two))
                def _():
                    own_to_two(c + AHEAD).start()
            pass_edges(2, c)

        @pl.when(has_one)
        def _(c=c):
            own_to_pair(c).wait_recv()
            pass_edges(1, c)

        if c == 0:
            @pl.when(below)
            def _():
                own_edge(False).start()

            @pl.when(above)
            def _():
                own_edge(True).start()

    for up, takes, gives in ((False, above, below), (True, below, above)):
        @pl.when(takes)
        def _(up=up):
            own_edge(up).wait_recv()

        @pl.when(gives)
        def _(up=up):
            own_edge(up).wait_send()
        for step, have in ((2, has_two), (1, has_one)):
            for c in range(CHUNKS):
                @pl.when(jnp.logical_and(takes, have))
                def _(up=up, step=step, c=c):
                    edge(step, up, c).wait_recv()

                @pl.when(jnp.logical_and(gives, have))
                def _(up=up, step=step, c=c):
                    edge(step, up, c).wait_send()
    for step in (1, 2):
        @pl.when(w + step < wides)
        def _(step=step):
            corner_copy(step).wait_recv()

        @pl.when(w >= step)
        def _(step=step):
            corner_copy(step).wait_send()
    for c in range(CHUNKS):
        @pl.when(gives_two)
        def _(c=c):
            own_to_two(c).wait_send()

        @pl.when(jnp.logical_or(is_odd, has_two))
        def _(c=c):
            own_to_pair(c).wait_send()
    own_copy.wait()
    corner_copy_own.wait()


def exchange_kernel(
    quads, slots, pool, corner_s, table, seg, dens, moved, pot_a, pot_b, final, prod,
):
    total_orbs, wide_rows, flat = pool.shape
    owned = total_orbs // 3
    planes = wide_rows - 2 * EDGE
    tiles = flat // LANES
    rows_y = flat // BZ
    w = lax.axis_index("wide")
    q = lax.axis_index("quad")

    lane = lax.broadcasted_iota(jnp.int32, (wide_rows, LANES), 1)
    zpos = lax.rem(lane, BZ)
    ylow = lane // BZ
    plane = lax.broadcasted_iota(jnp.int32, (wide_rows, LANES), 0) + (q * planes - EDGE)
    in_box = (plane >= 0) & (plane < quads * planes)

    def slot_facts(s):
        left = s % owned
        right = jnp.clip(corner_s[0, owned, s] - w * owned, 0, 3 * owned - 1)
        live = corner_s[0, owned + 1, s] != 0
        who, which = right // owned, lax.rem(right, owned)
        dy = corner_s[who, which, 0] - corner_s[0, left, 0]
        dz = corner_s[who, which, 1] - corner_s[0, left, 1]
        dy = jnp.clip(jnp.where(live, dy, 0), -SPAN, SPAN)
        dz = jnp.clip(jnp.where(live, dz, 0), -SPAN, SPAN)
        return left, right, live, dy, dz

    def mover(dy, dz, ok, rows):
        by = dy * BZ + dz
        whole = by >> 7
        rest = by & (LANES - 1)
        near_part = lane[:rows] < LANES - rest
        zfrom = zpos[:rows] - dz
        keep_z = (zfrom >= 0) & (zfrom < BZ) & ok
        yfrom = ylow[:rows] - dy

        def move(load, r):
            here = load(jnp.clip(r - whole, 0, tiles - 1))
            before = load(jnp.clip(r - whole - 1, 0, tiles - 1))
            turned = pltpu.roll(jnp.where(near_part, here, before), rest, 1)
            source = yfrom + 2 * r
            keep = keep_z & (source >= 0) & (source < rows_y)
            return jnp.where(keep, turned, 0.0)

        return move

    def column(t):
        return pl.ds(pl.multiple_of(t * LANES, LANES), LANES)

    half = tiles // 2
    factor = table[LANES:LANES + 8]

    def transform(rows):
        return jnp.dot(
            rows, table[0:LANES], precision=lax.Precision.HIGHEST,
            preferred_element_type=jnp.float32,
        )

    def regroup(a, b):
        low = lane[:a.shape[0]] < BZ
        return (
            jnp.where(low, a, pltpu.roll(b, BZ, 1)), jnp.where(low, pltpu.roll(a, BZ, 1), b)
        )

    def guard(field):
        rows = pl.ds(LOW - EDGE, wide_rows)
        field[0, rows] = jnp.where(lane >= BZ, pltpu.roll(field[tiles, rows], BZ, 1), 0.0)
        field[tiles + 1, rows] = jnp.where(lane < BZ, pltpu.roll(field[1, rows], BZ, 1), 0.0)

    facts = [slot_facts(s) for s in range(slots)]
    for s in range(slots):
        left, right, live, dy, dz = facts[s]
        move = mover(dy, dz, live, wide_rows)

        def two_tiles(i, carry, s=s, left=left, right=right, move=move):
            parts = []
            for r in (i, i + half):
                there = move(lambda t: pool[right, :, column(t)], r)
                moved[s, r] = there[EDGE:EDGE + planes]
                parts.append(jnp.where(in_box, there * pool[left, :, column(r)], 0.0))
            first, second = regroup(*parts)
            dens[s, 2 * i + 1, LOW - EDGE:LOW + planes + EDGE] = first
            dens[s, 2 * i + 2, LOW - EDGE:LOW + planes + EDGE] = second
            return carry

        lax.fori_loop(0, half, two_tiles, 0, unroll=2)

        def to_waves(i, carry, s=s):
            at = (s, pl.ds(1 + i * BLOCK, BLOCK), pl.ds(LOW - EDGE, wide_rows))
            rows = dens[at].reshape(BLOCK * wide_rows, LANES)
            dens[at] = transform(rows).reshape(BLOCK, wide_rows, LANES)
            return carry

        lax.fori_loop(0, tiles // BLOCK, to_waves, 0)
        guard(dens.at[s])

    weights = sweep_weights()
    pots = (pot_a, pot_b)
    nothing = jnp.minimum(w, 0)

    def one_slot(s, carry):
        for k in range(1, SWEEPS):
            gain = weights[k] / 6.5
            if k == 1:
                read = lambda t, first, size: dens[s, t, pl.ds(first, size)]
            else:
                read = lambda t, first, size, k=k: pots[k % 2][t, pl.ds(first, size)]
            last = k == SWEEPS - 1

            first, size = (LOW, planes) if last else (LOW - EDGE, wide_rows)
            if k == 1:
                start = weights[0] / 6.5
                keep = (1.0 - weights[1]) * start + gain + gain * start * factor
                gain = gain * start
            else:
                keep = (1.0 - weights[k]) + gain * factor
            keep = jnp.concatenate([keep] * (size // 8))

            def some_tiles(i, inner, k=k, gain=gain, read=read, last=last, keep=keep, first=first, size=size):
                r = i * GROUP
                next_row = first + 1 + nothing
                last_row = first - 1 + nothing
                here = [read(r + g, first, size) for g in range(GROUP + 2)]
                news = []
                for g in range(GROUP):
                    total = read(r + g + 1, next_row, size) + read(r + g + 1, last_row, size)
                    total = total + (here[g] + here[g + 2])
                    if k > 1:
                        total = total + dens[s, r + g + 1, pl.ds(first, size)]
                    new = keep * here[g + 1] + gain * total
                    if not last:
                        new = jnp.where(in_box, new, 0.0)
                    news.append(new)
                for g in range(GROUP):
                    pots[(k + 1) % 2][r + g + 1, pl.ds(first, size)] = news[g]
                return inner

            lax.fori_loop(0, tiles // GROUP, some_tiles, 0)
            if not last:
                guard(pots[(k + 1) % 2])

        def to_cells(i, inner):
            at = (pl.ds(1 + i * BLOCK, BLOCK), pl.ds(LOW, planes))
            rows = pots[SWEEPS % 2][at].reshape(BLOCK * planes, LANES)
            cells = transform(rows).reshape(BLOCK, planes, LANES)
            for g in range(0, BLOCK, 2):
                t = i * (BLOCK // 2) + g // 2
                for place, value in zip((t, t + half), regroup(cells[g], cells[g + 1])):
                    final[s, place] = value
                    own = pool[lax.rem(s, owned), EDGE:EDGE + planes, column(place)]
                    prod[s, place] = value * own
            return inner

        lax.fori_loop(0, tiles // BLOCK, to_cells, 0)
        return carry

    lax.fori_loop(0, slots, one_slot, 0)

    backs = [mover(-dy, -dz, live, planes) for left, right, live, dy, dz in facts]

    def terms(r, carry):
        total = [jnp.zeros((planes, LANES), jnp.float32) for o in range(3 * owned)]
        for s in range(slots):
            left, right = facts[s][:2]
            total[left] = total[left] + final[s, r] * moved[s, r]
            term = backs[s](lambda t: prod[s, t], r)
            for o in range(left + 1, min(left + 1 + REACH, 3 * owned)):
                total[o] = total[o] + jnp.where(right == o, term, 0.0)
        for o in range(3 * owned):
            seg[o, :, column(r)] = total[o]
        return carry

    lax.fori_loop(0, tiles, terms, 0, unroll=2)


def return_kernel(
    wides, seg, out, own, two, from_pair, from_two,
    local_sem, send_one, recv_one, send_two, recv_two,
):
    owned, planes, flat = out.shape
    chunk_width = flat // CHUNKS
    w = lax.axis_index("wide")
    odd = lax.rem(w, 2)
    is_odd = odd == 1
    is_even = odd == 0
    pair = w + 1 - 2 * odd
    has_two = w + 2 < wides
    takes_two = w >= 2
    sends_pair = jnp.logical_or(is_even, w + 1 < wides)
    takes_pair = jnp.logical_or(is_odd, has_two)
    even_two = jnp.logical_and(is_even, has_two)

    own_copy = pltpu.make_async_copy(seg.at[pl.ds(0, owned)], own, local_sem.at[0])
    two_copy = pltpu.make_async_copy(seg.at[pl.ds(2 * owned, owned)], two, local_sem.at[1])
    own_copy.start()
    two_copy.start()
    enter([
        (w >= 0, {"wide": pair}), (takes_two, {"wide": w - 2}), (has_two, {"wide": w + 2}),
    ])

    def columns(c):
        return pl.ds(c * chunk_width, chunk_width)

    def back_to_pair(c):
        return remote(
            seg.at[pl.ds(owned, owned), :, columns(c)], from_pair.at[:, :, columns(c)],
            send_one.at[c], recv_one.at[c], {"wide": pair},
        )

    def back_to_two(c):
        return remote(
            two.at[:, :, columns(c)], from_two.at[:, :, columns(c)],
            send_two.at[c], recv_two.at[c], {"wide": w + 2},
        )

    two_copy.wait()
    for c in range(CHUNKS):
        @pl.when(jnp.logical_and(sends_pair, jnp.logical_not(even_two)))
        def _(c=c):
            back_to_pair(c).start()

        @pl.when(jnp.logical_and(is_odd, has_two))
        def _(c=c):
            back_to_two(c).start()
    for c in range(CHUNKS):
        @pl.when(takes_pair)
        def _(c=c):
            back_to_pair(c).wait_recv()

        @pl.when(even_two)
        def _(c=c):
            two[:, :, columns(c)] += from_pair[:, :, columns(c)]
            back_to_two(c).start()
            back_to_pair(c).start()
    own_copy.wait()
    for c in range(CHUNKS):
        out[:, :, columns(c)] = own[:, :, columns(c)]

        @pl.when(is_odd)
        def _(c=c):
            out[:, :, columns(c)] += from_pair[:, :, columns(c)]

        @pl.when(takes_two)
        def _(c=c):
            back_to_two(c).wait_recv()
            out[:, :, columns(c)] += from_two[:, :, columns(c)]
    for c in range(CHUNKS):
        @pl.when(sends_pair)
        def _(c=c):
            back_to_pair(c).wait_send()

        @pl.when(has_two)
        def _(c=c):
            back_to_two(c).wait_send()


def per_device(wides, quads, orbitals, corners, pair_partner, pair_live):
    owned, planes, flat = orbitals.shape
    slots = pair_partner.shape[0]
    tiles = flat // LANES
    field_rows = planes + 2 * LOW
    corner_block = jnp.pad(corners, ((0, 8 - owned), (0, LANES - corners.shape[1])))
    for row, facts in ((owned, pair_partner), (owned + 1, pair_live)):
        corner_block += jnp.pad(facts[None], ((row, 7 - row), (0, LANES - slots)))
    f32 = jnp.float32
    dma = pltpu.SemaphoreType.DMA
    vmem = pl.BlockSpec(memory_space=pltpu.VMEM)
    smem = pl.BlockSpec(memory_space=pltpu.SMEM)
    anywhere = pl.BlockSpec(memory_space=pl.ANY)
    limit = 32 * 1024 * 1024
    pool, pool_corner = pl.pallas_call(
        functools.partial(gather_kernel, wides, quads),
        out_shape=(
            jax.ShapeDtypeStruct((3 * owned, planes + 2 * EDGE, flat), f32),
            jax.ShapeDtypeStruct((3, 8, LANES), jnp.int32),
        ),
        in_specs=[anywhere, anywhere],
        out_specs=(anywhere, anywhere),
        scratch_shapes=[
            dma((2,)), dma((2,)), dma((2,)),
            dma((CHUNKS,)), dma((CHUNKS,)), dma((CHUNKS,)), dma((CHUNKS,)),
            dma((2, 2, CHUNKS)), dma((2, 2, CHUNKS)), dma((2,)), dma((2,)),
        ],
        compiler_params=pltpu.CompilerParams(
            collective_id=0, has_side_effects=True, vmem_limit_bytes=limit
        ),
        name="gather",
    )(orbitals, corner_block)
    seg = pl.pallas_call(
        functools.partial(exchange_kernel, quads, slots),
        out_shape=jax.ShapeDtypeStruct((3 * owned, planes, flat), f32),
        in_specs=[vmem, smem, vmem],
        out_specs=vmem,
        scratch_shapes=[
            pltpu.VMEM((slots, tiles + 2, field_rows, LANES), f32),
            pltpu.VMEM((slots, tiles, planes, LANES), f32),
            pltpu.VMEM((tiles + 2, field_rows, LANES), f32),
            pltpu.VMEM((tiles + 2, field_rows, LANES), f32),
            pltpu.VMEM((slots, tiles, planes, LANES), f32),
            pltpu.VMEM((slots, tiles, planes, LANES), f32),
        ],
        compiler_params=pltpu.CompilerParams(vmem_limit_bytes=limit),
        name="exchange",
    )(pool, pool_corner, jnp.asarray(sine_table()))
    return pl.pallas_call(
        functools.partial(return_kernel, wides),
        out_shape=jax.ShapeDtypeStruct(orbitals.shape, f32),
        in_specs=[anywhere],
        out_specs=vmem,
        scratch_shapes=[
            pltpu.VMEM((owned, planes, flat), f32),
            pltpu.VMEM((owned, planes, flat), f32),
            pltpu.VMEM((owned, planes, flat), f32),
            pltpu.VMEM((owned, planes, flat), f32),
            dma((2,)), dma((CHUNKS,)), dma((CHUNKS,)), dma((CHUNKS,)), dma((CHUNKS,)),
        ],
        compiler_params=pltpu.CompilerParams(
            collective_id=1, has_side_effects=True, vmem_limit_bytes=limit
        ),
        name="give_back",
    )(seg)


def solution(mesh):
    in_specs = (P("wide", "quad", None), P("wide", None), P("wide"), P("wide"))
    out_specs = P("wide", "quad", None)
    body = functools.partial(per_device, mesh.shape["wide"], mesh.shape["quad"])
    return jax.shard_map(
        body, mesh=mesh, in_specs=in_specs, out_specs=out_specs, check_vma=False
    )
```

```python
import functools
import math

import jax
import jax.numpy as jnp
import numpy as np
from jax import lax
from jax.experimental import pallas as pl
from jax.experimental.pallas import tpu as pltpu
from jax.sharding import PartitionSpec as P

BZ = 64
SPAN = 16
SWEEPS = 8
REACH = 4
LANES = 128
EDGE = 8
LOW = 16
CHUNKS = 8
AHEAD = 2
BLOCK = 8
GROUP = 4
MESH = pl.DeviceIdType.MESH


def sweep_weights():
    low = 0.5 / 6.5
    high = 12.5 / 6.5
    center = (high + low) / 2.0
    half = (high - low) / 2.0
    return [
        1.0 / (center + half * math.cos(math.pi * (2 * k + 1) / (2 * SWEEPS)))
        for k in range(SWEEPS)
    ]


def sine_table():
    count = np.arange(1, BZ + 1)
    sine = np.sqrt(2.0 / (BZ + 1)) * np.sin(np.pi * np.outer(count, count) / (BZ + 1))
    both = np.kron(np.eye(LANES // BZ), sine)
    factor = np.tile(2.0 * np.cos(np.pi * count / (BZ + 1)), LANES // BZ)
    return np.concatenate([both, np.tile(factor, (8, 1))]).astype(np.float32)


def remote(src, dst, send, recv, target):
    return pltpu.make_async_remote_copy(
        src_ref=src, dst_ref=dst, send_sem=send, recv_sem=recv,
        device_id=target, device_id_type=MESH,
    )


def enter(near):
    barrier = pltpu.get_barrier_semaphore()
    for there, target in near:
        @pl.when(there)
        def _(target=target):
            pl.semaphore_signal(barrier, inc=1, device_id=target, device_id_type=MESH)
    count = jnp.int32(0)
    for there, target in near:
        count = count + jnp.where(there, 1, 0)
    pl.semaphore_wait(barrier, count)


def gather_kernel(
    wides, quads, orb, corner_in, pool, corner,
    local_sem, corner_send, corner_recv, send_two, recv_two, send_one, recv_one,
    edge_send, edge_recv, own_send, own_recv,
):
    owned, planes, flat = orb.shape
    chunk_width = flat // CHUNKS
    w = lax.axis_index("wide")
    q = lax.axis_index("quad")
    odd = lax.rem(w, 2)
    is_odd = odd == 1
    is_even = odd == 0
    pair = w + 1 - 2 * odd
    has_one = jnp.logical_or(is_even, w + 1 < wides)
    has_two = w + 2 < wides
    gives_two = w >= 2
    below = q >= 1
    above = q + 1 < quads
    enter([
        (w >= 1, {"wide": w - 1}), (gives_two, {"wide": w - 2}),
        (w + 1 < wides, {"wide": w + 1}), (has_two, {"wide": w + 2}),
        (below, {"quad": q - 1}), (above, {"quad": q + 1}),
    ])

    def columns(c):
        return pl.ds(c * chunk_width, chunk_width)

    def held(step, c):
        return pool.at[pl.ds(step * owned, owned), pl.ds(EDGE, planes), columns(c)]

    def corner_copy(step):
        return remote(
            corner_in, corner.at[step], corner_send.at[step - 1], corner_recv.at[step - 1],
            {"wide": w - step},
        )

    def own_to_two(c):
        return remote(
            orb.at[:, :, columns(c)], held(2, c), send_two.at[c], recv_two.at[c],
            {"wide": w - 2},
        )

    def own_to_pair(c):
        return remote(
            orb.at[:, :, columns(c)], held(1, c), send_one.at[c], recv_one.at[c],
            {"wide": pair},
        )

    def two_to_pair(c):
        return remote(held(2, c), held(1, c), send_one.at[c], recv_one.at[c], {"wide": pair})

    def own_edge(up):
        if up:
            return remote(
                orb.at[:, pl.ds(planes - EDGE, EDGE)],
                pool.at[pl.ds(0, owned), pl.ds(0, EDGE)],
                own_send.at[1], own_recv.at[1], {"quad": q + 1},
            )
        return remote(
            orb.at[:, pl.ds(0, EDGE)],
            pool.at[pl.ds(0, owned), pl.ds(EDGE + planes, EDGE)],
            own_send.at[0], own_recv.at[0], {"quad": q - 1},
        )

    def edge(step, up, c):
        rows = pl.ds(step * owned, owned)
        if up:
            src, dst, to = planes, 0, q + 1
        else:
            src, dst, to = EDGE, EDGE + planes, q - 1
        return remote(
            pool.at[rows, pl.ds(src, EDGE), columns(c)],
            pool.at[rows, pl.ds(dst, EDGE), columns(c)],
            edge_send.at[step - 1, int(up), c], edge_recv.at[step - 1, int(up), c],
            {"quad": to},
        )

    own_copy = pltpu.make_async_copy(
        orb, pool.at[pl.ds(0, owned), pl.ds(EDGE, planes)], local_sem.at[0]
    )
    corner_copy_own = pltpu.make_async_copy(corner_in, corner.at[0], local_sem.at[1])
    for step in (1, 2):
        @pl.when(w >= step)
        def _(step=step):
            corner_copy(step).start()
    own_copy.start()
    corner_copy_own.start()

    def pass_edges(step, c):
        @pl.when(below)
        def _():
            edge(step, False, c).start()

        @pl.when(above)
        def _():
            edge(step, True, c).start()

    for step in range(CHUNKS + 2 * AHEAD):
        if step < CHUNKS:
            if step >= AHEAD:
                @pl.when(gives_two)
                def _(c=step - AHEAD):
                    own_to_two(c).wait_send()

                @pl.when(is_odd)
                def _(c=step - AHEAD):
                    own_to_pair(c).wait_send()

            @pl.when(gives_two)
            def _(c=step):
                own_to_two(c).start()

            @pl.when(is_odd)
            def _(c=step):
                own_to_pair(c).start()
        if step == 0:
            @pl.when(below)
            def _():
                own_edge(False).start()

            @pl.when(above)
            def _():
                own_edge(True).start()
        if 0 <= step - AHEAD < CHUNKS:
            @pl.when(has_two)
            def _(c=step - AHEAD):
                own_to_two(c).wait_recv()

                @pl.when(is_even)
                def _():
                    two_to_pair(c).start()
                pass_edges(2, c)
        if 0 <= step - 2 * AHEAD < CHUNKS:
            @pl.when(has_one)
            def _(c=step - 2 * AHEAD):
                own_to_pair(c).wait_recv()
                pass_edges(1, c)

    for up, takes, gives in ((False, above, below), (True, below, above)):
        @pl.when(takes)
        def _(up=up):
            own_edge(up).wait_recv()

        @pl.when(gives)
        def _(up=up):
            own_edge(up).wait_send()
        for step, have in ((2, has_two), (1, has_one)):
            for c in range(CHUNKS):
                @pl.when(jnp.logical_and(takes, have))
                def _(up=up, step=step, c=c):
                    edge(step, up, c).wait_recv()

                @pl.when(jnp.logical_and(gives, have))
                def _(up=up, step=step, c=c):
                    edge(step, up, c).wait_send()
    for step in (1, 2):
        @pl.when(w + step < wides)
        def _(step=step):
            corner_copy(step).wait_recv()

        @pl.when(w >= step)
        def _(step=step):
            corner_copy(step).wait_send()
    for c in range(CHUNKS):
        if c >= CHUNKS - AHEAD:
            @pl.when(gives_two)
            def _(c=c):
                own_to_two(c).wait_send()

            @pl.when(is_odd)
            def _(c=c):
                own_to_pair(c).wait_send()

        @pl.when(jnp.logical_and(is_even, has_two))
        def _(c=c):
            two_to_pair(c).wait_send()
    own_copy.wait()
    corner_copy_own.wait()


def exchange_kernel(
    quads, slots, pool, corner_s, table, seg, dens, moved, pot_a, pot_b, final, prod,
):
    total_orbs, wide_rows, flat = pool.shape
    owned = total_orbs // 3
    planes = wide_rows - 2 * EDGE
    tiles = flat // LANES
    rows_y = flat // BZ
    w = lax.axis_index("wide")
    q = lax.axis_index("quad")

    lane = lax.broadcasted_iota(jnp.int32, (wide_rows, LANES), 1)
    zpos = lax.rem(lane, BZ)
    ylow = lane // BZ
    plane = lax.broadcasted_iota(jnp.int32, (wide_rows, LANES), 0) + (q * planes - EDGE)
    in_box = (plane >= 0) & (plane < quads * planes)

    def slot_facts(s):
        left = s % owned
        right = jnp.clip(corner_s[0, owned, s] - w * owned, 0, 3 * owned - 1)
        live = corner_s[0, owned + 1, s] != 0
        who, which = right // owned, lax.rem(right, owned)
        dy = corner_s[who, which, 0] - corner_s[0, left, 0]
        dz = corner_s[who, which, 1] - corner_s[0, left, 1]
        dy = jnp.clip(jnp.where(live, dy, 0), -SPAN, SPAN)
        dz = jnp.clip(jnp.where(live, dz, 0), -SPAN, SPAN)
        return left, right, live, dy, dz

    def mover(dy, dz, ok, rows):
        by = dy * BZ + dz
        whole = by >> 7
        rest = by & (LANES - 1)
        near_part = lane[:rows] < LANES - rest
        zfrom = zpos[:rows] - dz
        keep_z = (zfrom >= 0) & (zfrom < BZ) & ok
        yfrom = ylow[:rows] - dy

        def move(load, r):
            here = load(jnp.clip(r - whole, 0, tiles - 1))
            before = load(jnp.clip(r - whole - 1, 0, tiles - 1))
            turned = pltpu.roll(jnp.where(near_part, here, before), rest, 1)
            source = yfrom + 2 * r
            keep = keep_z & (source >= 0) & (source < rows_y)
            return jnp.where(keep, turned, 0.0)

        return move

    def column(t):
        return pl.ds(pl.multiple_of(t * LANES, LANES), LANES)

    half = tiles // 2
    factor = table[LANES:LANES + 8]

    bf16, f32 = jnp.bfloat16, jnp.float32
    fine = table[0:LANES]
    coarse = fine.astype(bf16)
    rest = (fine - coarse.astype(f32)).astype(bf16)
    both = jnp.concatenate([coarse, rest], axis=1)

    def transform(rows):
        high = rows.astype(bf16)
        low = (rows - high.astype(f32)).astype(bf16)
        total = jnp.dot(high, both, preferred_element_type=f32)
        return total[:, :LANES] + (
            total[:, LANES:] + jnp.dot(low, coarse, preferred_element_type=f32)
        )

    def regroup(a, b):
        low = lane[:a.shape[0]] < BZ
        return (
            jnp.where(low, a, pltpu.roll(b, BZ, 1)), jnp.where(low, pltpu.roll(a, BZ, 1), b)
        )

    def guard(field):
        rows = pl.ds(LOW - EDGE, wide_rows)
        field[0, rows] = jnp.where(lane >= BZ, pltpu.roll(field[tiles, rows], BZ, 1), 0.0)
        field[tiles + 1, rows] = jnp.where(lane < BZ, pltpu.roll(field[1, rows], BZ, 1), 0.0)

    facts = [slot_facts(s) for s in range(slots)]
    for s in range(slots):
        left, right, live, dy, dz = facts[s]
        move = mover(dy, dz, live, wide_rows)

        def two_tiles(i, carry, s=s, left=left, right=right, move=move):
            parts = []
            for r in (i, i + half):
                there = move(lambda t: pool[right, :, column(t)], r)
                moved[s, r] = there[EDGE:EDGE + planes]
                parts.append(jnp.where(in_box, there * pool[left, :, column(r)], 0.0))
            first, second = regroup(*parts)
            dens[s, 2 * i + 1, LOW - EDGE:LOW + planes + EDGE] = first
            dens[s, 2 * i + 2, LOW - EDGE:LOW + planes + EDGE] = second
            return carry

        lax.fori_loop(0, half, two_tiles, 0, unroll=2)

        def to_waves(i, carry, s=s):
            at = (s, pl.ds(1 + i * BLOCK, BLOCK), pl.ds(LOW - EDGE, wide_rows))
            rows = dens[at].reshape(BLOCK * wide_rows, LANES)
            dens[at] = transform(rows).reshape(BLOCK, wide_rows, LANES)
            return carry

        lax.fori_loop(0, tiles // BLOCK, to_waves, 0)
        guard(dens.at[s])

    weights = sweep_weights()
    pots = (pot_a, pot_b)
    nothing = jnp.minimum(w, 0)

    def one_slot(s, carry):
        for k in range(1, SWEEPS):
            gain = weights[k] / 6.5
            if k == 1:
                read = lambda t, first, size: dens[s, t, pl.ds(first, size)]
            else:
                read = lambda t, first, size, k=k: pots[k % 2][t, pl.ds(first, size)]
            last = k == SWEEPS - 1

            first, size = (LOW, planes) if last else (LOW - EDGE, wide_rows)
            if k == 1:
                start = weights[0] / 6.5
                keep = (1.0 - weights[1]) * start + gain + gain * start * factor
                gain = gain * start
            else:
                keep = (1.0 - weights[k]) + gain * factor
            keep = jnp.concatenate([keep] * (size // 8))

            def some_tiles(i, inner, k=k, gain=gain, read=read, last=last, keep=keep, first=first, size=size):
                r = i * GROUP
                next_row = first + 1 + nothing
                last_row = first - 1 + nothing
                here = [read(r + g, first, size) for g in range(GROUP + 2)]
                news = []
                for g in range(GROUP):
                    total = read(r + g + 1, next_row, size) + read(r + g + 1, last_row, size)
                    total = total + (here[g] + here[g + 2])
                    if k > 1:
                        total = total + dens[s, r + g + 1, pl.ds(first, size)]
                    new = keep * here[g + 1] + gain * total
                    if not last:
                        new = jnp.where(in_box, new, 0.0)
                    news.append(new)
                for g in range(GROUP):
                    pots[(k + 1) % 2][r + g + 1, pl.ds(first, size)] = news[g]
                return inner

            lax.fori_loop(0, tiles // GROUP, some_tiles, 0)
            if not last:
                guard(pots[(k + 1) % 2])

        def to_cells(i, inner):
            at = (pl.ds(1 + i * BLOCK, BLOCK), pl.ds(LOW, planes))
            rows = pots[SWEEPS % 2][at].reshape(BLOCK * planes, LANES)
            cells = transform(rows).reshape(BLOCK, planes, LANES)
            for g in range(0, BLOCK, 2):
                t = i * (BLOCK // 2) + g // 2
                for place, value in zip((t, t + half), regroup(cells[g], cells[g + 1])):
                    final[s, place] = value
                    own = pool[lax.rem(s, owned), EDGE:EDGE + planes, column(place)]
                    prod[s, place] = value * own
            return inner

        lax.fori_loop(0, tiles // BLOCK, to_cells, 0)
        return carry

    lax.fori_loop(0, slots, one_slot, 0)

    backs = [mover(-dy, -dz, live, planes) for left, right, live, dy, dz in facts]

    def terms(r, carry):
        total = [jnp.zeros((planes, LANES), jnp.float32) for o in range(3 * owned)]
        for s in range(slots):
            left, right = facts[s][:2]
            total[left] = total[left] + final[s, r] * moved[s, r]
            term = backs[s](lambda t: prod[s, t], r)
            for o in range(left + 1, min(left + 1 + REACH, 3 * owned)):
                total[o] = total[o] + jnp.where(right == o, term, 0.0)
        for o in range(3 * owned):
            seg[o, :, column(r)] = total[o]
        return carry

    lax.fori_loop(0, tiles, terms, 0, unroll=2)


def return_kernel(
    wides, seg, out, own, two, from_pair, from_two,
    local_sem, send_one, recv_one, send_two, recv_two,
):
    owned, planes, flat = out.shape
    chunk_width = flat // CHUNKS
    w = lax.axis_index("wide")
    odd = lax.rem(w, 2)
    is_odd = odd == 1
    is_even = odd == 0
    pair = w + 1 - 2 * odd
    has_two = w + 2 < wides
    takes_two = w >= 2
    takes_pair = jnp.logical_or(is_odd, has_two)
    even_two = jnp.logical_and(is_even, has_two)

    own_copy = pltpu.make_async_copy(seg.at[pl.ds(0, owned)], own, local_sem.at[0])
    two_copy = pltpu.make_async_copy(seg.at[pl.ds(2 * owned, owned)], two, local_sem.at[1])
    own_copy.start()
    two_copy.start()
    enter([
        (w >= 0, {"wide": pair}), (takes_two, {"wide": w - 2}), (has_two, {"wide": w + 2}),
    ])

    def columns(c):
        return pl.ds(c * chunk_width, chunk_width)

    def back_to_pair(c):
        return remote(
            seg.at[pl.ds(owned, owned), :, columns(c)], from_pair.at[:, :, columns(c)],
            send_one.at[c], recv_one.at[c], {"wide": pair},
        )

    def back_to_two(c):
        return remote(
            two.at[:, :, columns(c)], from_two.at[:, :, columns(c)],
            send_two.at[c], recv_two.at[c], {"wide": w + 2},
        )

    two_copy.wait()
    for c in range(CHUNKS):
        if c >= AHEAD:
            @pl.when(jnp.logical_and(is_odd, has_two))
            def _(c=c - AHEAD):
                back_to_pair(c).wait_send()
                back_to_two(c).wait_send()

        @pl.when(jnp.logical_and(is_odd, has_two))
        def _(c=c):
            back_to_pair(c).start()
            back_to_two(c).start()

        @pl.when(jnp.logical_and(is_even, jnp.logical_not(has_two)))
        def _(c=c):
            back_to_pair(c).start()
    for c in range(CHUNKS):
        @pl.when(takes_pair)
        def _(c=c):
            back_to_pair(c).wait_recv()

        @pl.when(even_two)
        def _(c=c):
            two[:, :, columns(c)] += from_pair[:, :, columns(c)]
            back_to_two(c).start()
            back_to_pair(c).start()
    own_copy.wait()
    for c in range(CHUNKS):
        out[:, :, columns(c)] = own[:, :, columns(c)]

        @pl.when(is_odd)
        def _(c=c):
            out[:, :, columns(c)] += from_pair[:, :, columns(c)]

        @pl.when(takes_two)
        def _(c=c):
            back_to_two(c).wait_recv()
            out[:, :, columns(c)] += from_two[:, :, columns(c)]
    for c in range(CHUNKS):
        @pl.when(is_even)
        def _(c=c):
            back_to_pair(c).wait_send()

        @pl.when(even_two)
        def _(c=c):
            back_to_two(c).wait_send()
        if c >= CHUNKS - AHEAD:
            @pl.when(jnp.logical_and(is_odd, has_two))
            def _(c=c):
                back_to_pair(c).wait_send()
                back_to_two(c).wait_send()


def per_device(wides, quads, orbitals, corners, pair_partner, pair_live):
    owned, planes, flat = orbitals.shape
    slots = pair_partner.shape[0]
    tiles = flat // LANES
    field_rows = planes + 2 * LOW
    corner_block = jnp.pad(corners, ((0, 8 - owned), (0, LANES - corners.shape[1])))
    for row, facts in ((owned, pair_partner), (owned + 1, pair_live)):
        corner_block += jnp.pad(facts[None], ((row, 7 - row), (0, LANES - slots)))
    f32 = jnp.float32
    dma = pltpu.SemaphoreType.DMA
    vmem = pl.BlockSpec(memory_space=pltpu.VMEM)
    smem = pl.BlockSpec(memory_space=pltpu.SMEM)
    anywhere = pl.BlockSpec(memory_space=pl.ANY)
    limit = 32 * 1024 * 1024
    pool, pool_corner = pl.pallas_call(
        functools.partial(gather_kernel, wides, quads),
        out_shape=(
            jax.ShapeDtypeStruct((3 * owned, planes + 2 * EDGE, flat), f32),
            jax.ShapeDtypeStruct((3, 8, LANES), jnp.int32),
        ),
        in_specs=[anywhere, anywhere],
        out_specs=(anywhere, anywhere),
        scratch_shapes=[
            dma((2,)), dma((2,)), dma((2,)),
            dma((CHUNKS,)), dma((CHUNKS,)), dma((CHUNKS,)), dma((CHUNKS,)),
            dma((2, 2, CHUNKS)), dma((2, 2, CHUNKS)), dma((2,)), dma((2,)),
        ],
        compiler_params=pltpu.CompilerParams(
            collective_id=0, has_side_effects=True, vmem_limit_bytes=limit
        ),
        name="gather",
    )(orbitals, corner_block)
    seg = pl.pallas_call(
        functools.partial(exchange_kernel, quads, slots),
        out_shape=jax.ShapeDtypeStruct((3 * owned, planes, flat), f32),
        in_specs=[vmem, smem, vmem],
        out_specs=vmem,
        scratch_shapes=[
            pltpu.VMEM((slots, tiles + 2, field_rows, LANES), f32),
            pltpu.VMEM((slots, tiles, planes, LANES), f32),
            pltpu.VMEM((tiles + 2, field_rows, LANES), f32),
            pltpu.VMEM((tiles + 2, field_rows, LANES), f32),
            pltpu.VMEM((slots, tiles, planes, LANES), f32),
            pltpu.VMEM((slots, tiles, planes, LANES), f32),
        ],
        compiler_params=pltpu.CompilerParams(vmem_limit_bytes=limit),
        name="exchange",
    )(pool, pool_corner, jnp.asarray(sine_table()))
    return pl.pallas_call(
        functools.partial(return_kernel, wides),
        out_shape=jax.ShapeDtypeStruct(orbitals.shape, f32),
        in_specs=[anywhere],
        out_specs=vmem,
        scratch_shapes=[
            pltpu.VMEM((owned, planes, flat), f32),
            pltpu.VMEM((owned, planes, flat), f32),
            pltpu.VMEM((owned, planes, flat), f32),
            pltpu.VMEM((owned, planes, flat), f32),
            dma((2,)), dma((CHUNKS,)), dma((CHUNKS,)), dma((CHUNKS,)), dma((CHUNKS,)),
        ],
        compiler_params=pltpu.CompilerParams(
            collective_id=1, has_side_effects=True, vmem_limit_bytes=limit
        ),
        name="give_back",
    )(seg)


def solution(mesh):
    in_specs = (P("wide", "quad", None), P("wide", None), P("wide"), P("wide"))
    out_specs = P("wide", "quad", None)
    body = functools.partial(per_device, mesh.shape["wide"], mesh.shape["quad"])
    return jax.shard_map(
        body, mesh=mesh, in_specs=in_specs, out_specs=out_specs, check_vma=False
    )
```

```python
import functools
import math

import jax
import jax.numpy as jnp
import numpy as np
from jax import lax
from jax.experimental import pallas as pl
from jax.experimental.pallas import tpu as pltpu
from jax.sharding import PartitionSpec as P

BZ = 64
SPAN = 16
SWEEPS = 8
REACH = 4
LANES = 128
EDGE = 8
LOW = 16
CHUNKS = 8
AHEAD = 2
BLOCK = 8
GROUP = 4
MESH = pl.DeviceIdType.MESH


def sweep_weights():
    low = 0.5 / 6.5
    high = 12.5 / 6.5
    center = (high + low) / 2.0
    half = (high - low) / 2.0
    return [
        1.0 / (center + half * math.cos(math.pi * (2 * k + 1) / (2 * SWEEPS)))
        for k in range(SWEEPS)
    ]


def sine_table():
    count = np.arange(1, BZ + 1)
    sine = np.sqrt(2.0 / (BZ + 1)) * np.sin(np.pi * np.outer(count, count) / (BZ + 1))
    both = np.kron(np.eye(LANES // BZ), sine)
    factor = np.tile(2.0 * np.cos(np.pi * count / (BZ + 1)), LANES // BZ)
    return np.concatenate([both, np.tile(factor, (8, 1))]).astype(np.float32)


def remote(src, dst, send, recv, target):
    return pltpu.make_async_remote_copy(
        src_ref=src, dst_ref=dst, send_sem=send, recv_sem=recv,
        device_id=target, device_id_type=MESH,
    )


def enter(near):
    barrier = pltpu.get_barrier_semaphore()
    for there, target in near:
        @pl.when(there)
        def _(target=target):
            pl.semaphore_signal(barrier, inc=1, device_id=target, device_id_type=MESH)
    count = jnp.int32(0)
    for there, target in near:
        count = count + jnp.where(there, 1, 0)
    pl.semaphore_wait(barrier, count)


def gather_kernel(
    wides, quads, orb, corner_in, pool, corner,
    local_sem, corner_send, corner_recv, send_two, recv_two, send_one, recv_one,
    edge_send, edge_recv, own_send, own_recv,
):
    owned, planes, flat = orb.shape
    chunk_width = flat // CHUNKS
    w = lax.axis_index("wide")
    q = lax.axis_index("quad")
    odd = lax.rem(w, 2)
    is_odd = odd == 1
    is_even = odd == 0
    pair = w + 1 - 2 * odd
    has_one = jnp.logical_or(is_even, w + 1 < wides)
    has_two = w + 2 < wides
    gives_two = w >= 2
    below = q >= 1
    above = q + 1 < quads
    enter([
        (w >= 1, {"wide": w - 1}), (gives_two, {"wide": w - 2}),
        (w + 1 < wides, {"wide": w + 1}), (has_two, {"wide": w + 2}),
        (below, {"quad": q - 1}), (above, {"quad": q + 1}),
    ])

    def columns(c):
        return pl.ds(c * chunk_width, chunk_width)

    def held(step, c):
        return pool.at[pl.ds(step * owned, owned), pl.ds(EDGE, planes), columns(c)]

    def corner_copy(step):
        return remote(
            corner_in, corner.at[step], corner_send.at[step - 1], corner_recv.at[step - 1],
            {"wide": w - step},
        )

    def own_to_two(c):
        return remote(
            orb.at[:, :, columns(c)], held(2, c), send_two.at[c], recv_two.at[c],
            {"wide": w - 2},
        )

    def own_to_pair(c):
        return remote(
            orb.at[:, :, columns(c)], held(1, c), send_one.at[c], recv_one.at[c],
            {"wide": pair},
        )

    def two_to_pair(c):
        return remote(held(2, c), held(1, c), send_one.at[c], recv_one.at[c], {"wide": pair})

    def own_edge(up):
        if up:
            return remote(
                orb.at[:, pl.ds(planes - EDGE, EDGE)],
                pool.at[pl.ds(0, owned), pl.ds(0, EDGE)],
                own_send.at[1], own_recv.at[1], {"quad": q + 1},
            )
        return remote(
            orb.at[:, pl.ds(0, EDGE)],
            pool.at[pl.ds(0, owned), pl.ds(EDGE + planes, EDGE)],
            own_send.at[0], own_recv.at[0], {"quad": q - 1},
        )

    def edge(step, up, c):
        rows = pl.ds(step * owned, owned)
        if up:
            src, dst, to = planes, 0, q + 1
        else:
            src, dst, to = EDGE, EDGE + planes, q - 1
        return remote(
            pool.at[rows, pl.ds(src, EDGE), columns(c)],
            pool.at[rows, pl.ds(dst, EDGE), columns(c)],
            edge_send.at[step - 1, int(up), c], edge_recv.at[step - 1, int(up), c],
            {"quad": to},
        )

    own_copy = pltpu.make_async_copy(
        orb, pool.at[pl.ds(0, owned), pl.ds(EDGE, planes)], local_sem.at[0]
    )
    corner_copy_own = pltpu.make_async_copy(corner_in, corner.at[0], local_sem.at[1])
    for step in (1, 2):
        @pl.when(w >= step)
        def _(step=step):
            corner_copy(step).start()
    own_copy.start()
    corner_copy_own.start()

    def pass_edges(step, c):
        @pl.when(below)
        def _():
            edge(step, False, c).start()

        @pl.when(above)
        def _():
            edge(step, True, c).start()

    for step in range(CHUNKS + 2 * AHEAD):
        if step < CHUNKS:
            if step >= AHEAD:
                @pl.when(gives_two)
                def _(c=step - AHEAD):
                    own_to_two(c).wait_send()

                @pl.when(is_odd)
                def _(c=step - AHEAD):
                    own_to_pair(c).wait_send()

            @pl.when(gives_two)
            def _(c=step):
                own_to_two(c).start()

            @pl.when(is_odd)
            def _(c=step):
                own_to_pair(c).start()
        if step == 0:
            @pl.when(below)
            def _():
                own_edge(False).start()

            @pl.when(above)
            def _():
                own_edge(True).start()
        if 0 <= step - AHEAD < CHUNKS:
            @pl.when(has_two)
            def _(c=step - AHEAD):
                own_to_two(c).wait_recv()

                @pl.when(is_even)
                def _():
                    two_to_pair(c).start()
                pass_edges(2, c)
        if 0 <= step - 2 * AHEAD < CHUNKS:
            @pl.when(has_one)
            def _(c=step - 2 * AHEAD):
                own_to_pair(c).wait_recv()
                pass_edges(1, c)

    for up, takes, gives in ((False, above, below), (True, below, above)):
        @pl.when(takes)
        def _(up=up):
            own_edge(up).wait_recv()

        @pl.when(gives)
        def _(up=up):
            own_edge(up).wait_send()
        for step, have in ((2, has_two), (1, has_one)):
            for c in range(CHUNKS):
                @pl.when(jnp.logical_and(takes, have))
                def _(up=up, step=step, c=c):
                    edge(step, up, c).wait_recv()

                @pl.when(jnp.logical_and(gives, have))
                def _(up=up, step=step, c=c):
                    edge(step, up, c).wait_send()
    for step in (1, 2):
        @pl.when(w + step < wides)
        def _(step=step):
            corner_copy(step).wait_recv()

        @pl.when(w >= step)
        def _(step=step):
            corner_copy(step).wait_send()
    for c in range(CHUNKS):
        if c >= CHUNKS - AHEAD:
            @pl.when(gives_two)
            def _(c=c):
                own_to_two(c).wait_send()

            @pl.when(is_odd)
            def _(c=c):
                own_to_pair(c).wait_send()

        @pl.when(jnp.logical_and(is_even, has_two))
        def _(c=c):
            two_to_pair(c).wait_send()
    own_copy.wait()
    corner_copy_own.wait()


def exchange_kernel(
    quads, slots, pool, corner_s, table, seg, dens, moved, pot_a, pot_b, final, prod,
):
    total_orbs, wide_rows, flat = pool.shape
    owned = total_orbs // 3
    planes = wide_rows - 2 * EDGE
    tiles = flat // LANES
    rows_y = flat // BZ
    w = lax.axis_index("wide")
    q = lax.axis_index("quad")

    lane = lax.broadcasted_iota(jnp.int32, (wide_rows, LANES), 1)
    zpos = lax.rem(lane, BZ)
    ylow = lane // BZ
    plane = lax.broadcasted_iota(jnp.int32, (wide_rows, LANES), 0) + (q * planes - EDGE)
    in_box = (plane >= 0) & (plane < quads * planes)

    def slot_facts(s):
        left = s % owned
        right = jnp.clip(corner_s[0, owned, s] - w * owned, 0, 3 * owned - 1)
        live = corner_s[0, owned + 1, s] != 0
        who, which = right // owned, lax.rem(right, owned)
        dy = corner_s[who, which, 0] - corner_s[0, left, 0]
        dz = corner_s[who, which, 1] - corner_s[0, left, 1]
        dy = jnp.clip(jnp.where(live, dy, 0), -SPAN, SPAN)
        dz = jnp.clip(jnp.where(live, dz, 0), -SPAN, SPAN)
        return left, right, live, dy, dz

    def mover(dy, dz, ok, rows):
        by = dy * BZ + dz
        whole = by >> 7
        rest = by & (LANES - 1)
        near_part = lane[:rows] < LANES - rest
        zfrom = zpos[:rows] - dz
        keep_z = (zfrom >= 0) & (zfrom < BZ) & ok
        yfrom = ylow[:rows] - dy

        def move(load, r):
            here = load(jnp.clip(r - whole, 0, tiles - 1))
            before = load(jnp.clip(r - whole - 1, 0, tiles - 1))
            turned = pltpu.roll(jnp.where(near_part, here, before), rest, 1)
            source = yfrom + 2 * r
            keep = keep_z & (source >= 0) & (source < rows_y)
            return jnp.where(keep, turned, 0.0)

        return move

    def column(t):
        return pl.ds(pl.multiple_of(t * LANES, LANES), LANES)

    half = tiles // 2
    factor = table[LANES:LANES + 8]

    bf16, f32 = jnp.bfloat16, jnp.float32
    fine = table[0:LANES]
    coarse = fine.astype(bf16)
    rest = (fine - coarse.astype(f32)).astype(bf16)
    both = jnp.concatenate([coarse, rest], axis=1)

    def transform(rows):
        high = rows.astype(bf16)
        low = (rows - high.astype(f32)).astype(bf16)
        total = jnp.dot(high, both, preferred_element_type=f32)
        return total[:, :LANES] + (
            total[:, LANES:] + jnp.dot(low, coarse, preferred_element_type=f32)
        )

    def regroup(a, b):
        low = lane[:a.shape[0]] < BZ
        return (
            jnp.where(low, a, pltpu.roll(b, BZ, 1)), jnp.where(low, pltpu.roll(a, BZ, 1), b)
        )

    def guard(field):
        rows = pl.ds(LOW - EDGE, wide_rows)
        field[0, rows] = jnp.where(lane >= BZ, pltpu.roll(field[tiles, rows], BZ, 1), 0.0)
        field[tiles + 1, rows] = jnp.where(lane < BZ, pltpu.roll(field[1, rows], BZ, 1), 0.0)

    facts = [slot_facts(s) for s in range(slots)]
    for s in range(slots):
        left, right, live, dy, dz = facts[s]
        move = mover(dy, dz, live, wide_rows)

        @pl.when(live)
        def _(s=s, left=left, right=right, move=move):
            def two_tiles(i, carry):
                parts = []
                for r in (i, i + half):
                    there = move(lambda t: pool[right, :, column(t)], r)
                    moved[s, r] = there[EDGE:EDGE + planes]
                    parts.append(jnp.where(in_box, there * pool[left, :, column(r)], 0.0))
                first, second = regroup(*parts)
                dens[s, 2 * i + 1, LOW - EDGE:LOW + planes + EDGE] = first
                dens[s, 2 * i + 2, LOW - EDGE:LOW + planes + EDGE] = second
                return carry

            lax.fori_loop(0, half, two_tiles, 0, unroll=2)

            def to_waves(i, carry):
                at = (s, pl.ds(1 + i * BLOCK, BLOCK), pl.ds(LOW - EDGE, wide_rows))
                rows = dens[at].reshape(BLOCK * wide_rows, LANES)
                dens[at] = transform(rows).reshape(BLOCK, wide_rows, LANES)
                return carry

            lax.fori_loop(0, tiles // BLOCK, to_waves, 0)
            guard(dens.at[s])

        @pl.when(jnp.logical_not(live))
        def _(s=s):
            def clear(r, carry):
                for field in (moved, final, prod):
                    field[s, r] = jnp.zeros((planes, LANES), jnp.float32)
                return carry

            lax.fori_loop(0, tiles, clear, 0, unroll=4)

    weights = sweep_weights()
    pots = (pot_a, pot_b)
    nothing = jnp.minimum(w, 0)

    def one_slot(s, carry):
        for k in range(1, SWEEPS):
            gain = weights[k] / 6.5
            if k == 1:
                read = lambda t, first, size: dens[s, t, pl.ds(first, size)]
            else:
                read = lambda t, first, size, k=k: pots[k % 2][t, pl.ds(first, size)]
            last = k == SWEEPS - 1

            first, size = (LOW, planes) if last else (LOW - EDGE, wide_rows)
            if k == 1:
                start = weights[0] / 6.5
                keep = (1.0 - weights[1]) * start + gain + gain * start * factor
                gain = gain * start
            else:
                keep = (1.0 - weights[k]) + gain * factor
            keep = jnp.concatenate([keep] * (size // 8))

            def some_tiles(i, inner, k=k, gain=gain, read=read, last=last, keep=keep, first=first, size=size):
                r = i * GROUP
                next_row = first + 1 + nothing
                last_row = first - 1 + nothing
                here = [read(r + g, first, size) for g in range(GROUP + 2)]
                news = []
                for g in range(GROUP):
                    total = read(r + g + 1, next_row, size) + read(r + g + 1, last_row, size)
                    total = total + (here[g] + here[g + 2])
                    if k > 1:
                        total = total + dens[s, r + g + 1, pl.ds(first, size)]
                    new = keep * here[g + 1] + gain * total
                    if not last:
                        new = jnp.where(in_box, new, 0.0)
                    news.append(new)
                for g in range(GROUP):
                    pots[(k + 1) % 2][r + g + 1, pl.ds(first, size)] = news[g]
                return inner

            lax.fori_loop(0, tiles // GROUP, some_tiles, 0)
            if not last:
                guard(pots[(k + 1) % 2])

        def to_cells(i, inner):
            at = (pl.ds(1 + i * BLOCK, BLOCK), pl.ds(LOW, planes))
            rows = pots[SWEEPS % 2][at].reshape(BLOCK * planes, LANES)
            cells = transform(rows).reshape(BLOCK, planes, LANES)
            for g in range(0, BLOCK, 2):
                t = i * (BLOCK // 2) + g // 2
                for place, value in zip((t, t + half), regroup(cells[g], cells[g + 1])):
                    final[s, place] = value
                    own = pool[lax.rem(s, owned), EDGE:EDGE + planes, column(place)]
                    prod[s, place] = value * own
            return inner

        lax.fori_loop(0, tiles // BLOCK, to_cells, 0)
        return carry

    def live_slot(s, carry):
        @pl.when(corner_s[0, owned + 1, s] != 0)
        def _():
            one_slot(s, 0)
        return carry

    lax.fori_loop(0, slots, live_slot, 0)

    backs = [mover(-dy, -dz, live, planes) for left, right, live, dy, dz in facts]

    def terms(r, carry):
        total = [jnp.zeros((planes, LANES), jnp.float32) for o in range(3 * owned)]
        for s in range(slots):
            left, right = facts[s][:2]
            total[left] = total[left] + final[s, r] * moved[s, r]
            term = backs[s](lambda t: prod[s, t], r)
            for o in range(left + 1, min(left + 1 + REACH, 3 * owned)):
                total[o] = total[o] + jnp.where(right == o, term, 0.0)
        for o in range(3 * owned):
            seg[o, :, column(r)] = total[o]
        return carry

    lax.fori_loop(0, tiles, terms, 0, unroll=2)


def return_kernel(
    wides, seg, out, own, two, from_pair, from_two,
    local_sem, send_one, recv_one, send_two, recv_two,
):
    owned, planes, flat = out.shape
    chunk_width = flat // CHUNKS
    w = lax.axis_index("wide")
    odd = lax.rem(w, 2)
    is_odd = odd == 1
    is_even = odd == 0
    pair = w + 1 - 2 * odd
    has_two = w + 2 < wides
    takes_two = w >= 2
    takes_pair = jnp.logical_or(is_odd, has_two)
    even_two = jnp.logical_and(is_even, has_two)

    own_copy = pltpu.make_async_copy(seg.at[pl.ds(0, owned)], own, local_sem.at[0])
    two_copy = pltpu.make_async_copy(seg.at[pl.ds(2 * owned, owned)], two, local_sem.at[1])
    own_copy.start()
    two_copy.start()
    enter([
        (w >= 0, {"wide": pair}), (takes_two, {"wide": w - 2}), (has_two, {"wide": w + 2}),
    ])

    def columns(c):
        return pl.ds(c * chunk_width, chunk_width)

    def back_to_pair(c):
        return remote(
            seg.at[pl.ds(owned, owned), :, columns(c)], from_pair.at[:, :, columns(c)],
            send_one.at[c], recv_one.at[c], {"wide": pair},
        )

    def back_to_two(c):
        return remote(
            two.at[:, :, columns(c)], from_two.at[:, :, columns(c)],
            send_two.at[c], recv_two.at[c], {"wide": w + 2},
        )

    two_copy.wait()
    for c in range(CHUNKS):
        if c >= AHEAD:
            @pl.when(jnp.logical_and(is_odd, has_two))
            def _(c=c - AHEAD):
                back_to_pair(c).wait_send()
                back_to_two(c).wait_send()

        @pl.when(jnp.logical_and(is_odd, has_two))
        def _(c=c):
            back_to_pair(c).start()
            back_to_two(c).start()

        @pl.when(jnp.logical_and(is_even, jnp.logical_not(has_two)))
        def _(c=c):
            back_to_pair(c).start()
    for c in range(CHUNKS):
        @pl.when(takes_pair)
        def _(c=c):
            back_to_pair(c).wait_recv()

        @pl.when(even_two)
        def _(c=c):
            two[:, :, columns(c)] += from_pair[:, :, columns(c)]
            back_to_two(c).start()
            back_to_pair(c).start()
    own_copy.wait()
    for c in range(CHUNKS):
        out[:, :, columns(c)] = own[:, :, columns(c)]

        @pl.when(is_odd)
        def _(c=c):
            out[:, :, columns(c)] += from_pair[:, :, columns(c)]

        @pl.when(takes_two)
        def _(c=c):
            back_to_two(c).wait_recv()
            out[:, :, columns(c)] += from_two[:, :, columns(c)]
    for c in range(CHUNKS):
        @pl.when(is_even)
        def _(c=c):
            back_to_pair(c).wait_send()

        @pl.when(even_two)
        def _(c=c):
            back_to_two(c).wait_send()
        if c >= CHUNKS - AHEAD:
            @pl.when(jnp.logical_and(is_odd, has_two))
            def _(c=c):
                back_to_pair(c).wait_send()
                back_to_two(c).wait_send()


def per_device(wides, quads, orbitals, corners, pair_partner, pair_live):
    owned, planes, flat = orbitals.shape
    slots = pair_partner.shape[0]
    tiles = flat // LANES
    field_rows = planes + 2 * LOW
    corner_block = jnp.pad(corners, ((0, 8 - owned), (0, LANES - corners.shape[1])))
    for row, facts in ((owned, pair_partner), (owned + 1, pair_live)):
        corner_block += jnp.pad(facts[None], ((row, 7 - row), (0, LANES - slots)))
    f32 = jnp.float32
    dma = pltpu.SemaphoreType.DMA
    vmem = pl.BlockSpec(memory_space=pltpu.VMEM)
    smem = pl.BlockSpec(memory_space=pltpu.SMEM)
    anywhere = pl.BlockSpec(memory_space=pl.ANY)
    limit = 32 * 1024 * 1024
    pool, pool_corner = pl.pallas_call(
        functools.partial(gather_kernel, wides, quads),
        out_shape=(
            jax.ShapeDtypeStruct((3 * owned, planes + 2 * EDGE, flat), f32),
            jax.ShapeDtypeStruct((3, 8, LANES), jnp.int32),
        ),
        in_specs=[pl.BlockSpec(memory_space=pltpu.HBM), anywhere],
        out_specs=(anywhere, anywhere),
        scratch_shapes=[
            dma((2,)), dma((2,)), dma((2,)),
            dma((CHUNKS,)), dma((CHUNKS,)), dma((CHUNKS,)), dma((CHUNKS,)),
            dma((2, 2, CHUNKS)), dma((2, 2, CHUNKS)), dma((2,)), dma((2,)),
        ],
        compiler_params=pltpu.CompilerParams(
            collective_id=0, has_side_effects=True, vmem_limit_bytes=limit
        ),
        name="gather",
    )(orbitals, corner_block)
    seg = pl.pallas_call(
        functools.partial(exchange_kernel, quads, slots),
        out_shape=jax.ShapeDtypeStruct((3 * owned, planes, flat), f32),
        in_specs=[vmem, smem, vmem],
        out_specs=vmem,
        scratch_shapes=[
            pltpu.VMEM((slots, tiles + 2, field_rows, LANES), f32),
            pltpu.VMEM((slots, tiles, planes, LANES), f32),
            pltpu.VMEM((tiles + 2, field_rows, LANES), f32),
            pltpu.VMEM((tiles + 2, field_rows, LANES), f32),
            pltpu.VMEM((slots, tiles, planes, LANES), f32),
            pltpu.VMEM((slots, tiles, planes, LANES), f32),
        ],
        compiler_params=pltpu.CompilerParams(vmem_limit_bytes=limit),
        name="exchange",
    )(pool, pool_corner, jnp.asarray(sine_table()))
    return pl.pallas_call(
        functools.partial(return_kernel, wides),
        out_shape=jax.ShapeDtypeStruct(orbitals.shape, f32),
        in_specs=[anywhere],
        out_specs=vmem,
        scratch_shapes=[
            pltpu.VMEM((owned, planes, flat), f32),
            pltpu.VMEM((owned, planes, flat), f32),
            pltpu.VMEM((owned, planes, flat), f32),
            pltpu.VMEM((owned, planes, flat), f32),
            dma((2,)), dma((CHUNKS,)), dma((CHUNKS,)), dma((CHUNKS,)), dma((CHUNKS,)),
        ],
        compiler_params=pltpu.CompilerParams(
            collective_id=1, has_side_effects=True, vmem_limit_bytes=limit
        ),
        name="give_back",
    )(seg)


def solution(mesh):
    in_specs = (P("wide", "quad", None), P("wide", None), P("wide"), P("wide"))
    out_specs = P("wide", "quad", None)
    body = functools.partial(per_device, mesh.shape["wide"], mesh.shape["quad"])
    return jax.shard_map(
        body, mesh=mesh, in_specs=in_specs, out_specs=out_specs, check_vma=False
    )
```

```python
import functools
import math

import jax
import jax.numpy as jnp
import numpy as np
from jax import lax
from jax.experimental import pallas as pl
from jax.experimental.pallas import tpu as pltpu
from jax.sharding import PartitionSpec as P

BZ = 64
SPAN = 16
SWEEPS = 8
REACH = 4
LANES = 128
EDGE = 8
LOW = 16
CHUNKS = 8
AHEAD = 2
BLOCK = 8
GROUP = 4
MESH = pl.DeviceIdType.MESH


def sweep_weights():
    low = 0.5 / 6.5
    high = 12.5 / 6.5
    center = (high + low) / 2.0
    half = (high - low) / 2.0
    return [
        1.0 / (center + half * math.cos(math.pi * (2 * k + 1) / (2 * SWEEPS)))
        for k in range(SWEEPS)
    ]


def sine_table():
    count = np.arange(1, BZ + 1)
    sine = np.sqrt(2.0 / (BZ + 1)) * np.sin(np.pi * np.outer(count, count) / (BZ + 1))
    both = np.kron(np.eye(LANES // BZ), sine)
    factor = np.tile(2.0 * np.cos(np.pi * count / (BZ + 1)), LANES // BZ)
    return np.concatenate([both, np.tile(factor, (8, 1))]).astype(np.float32)


def remote(src, dst, send, recv, target):
    return pltpu.make_async_remote_copy(
        src_ref=src, dst_ref=dst, send_sem=send, recv_sem=recv,
        device_id=target, device_id_type=MESH,
    )


def enter(near):
    barrier = pltpu.get_barrier_semaphore()
    for there, target in near:
        @pl.when(there)
        def _(target=target):
            pl.semaphore_signal(barrier, inc=1, device_id=target, device_id_type=MESH)
    count = jnp.int32(0)
    for there, target in near:
        count = count + jnp.where(there, 1, 0)
    pl.semaphore_wait(barrier, count)


def gather_kernel(
    wides, quads, orb, corner_in, pool, corner,
    local_sem, corner_send, corner_recv, send_two, recv_two, send_one, recv_one,
    edge_send, edge_recv, own_send, own_recv,
):
    owned, planes, flat = orb.shape
    chunk_width = flat // CHUNKS
    w = lax.axis_index("wide")
    q = lax.axis_index("quad")
    odd = lax.rem(w, 2)
    is_odd = odd == 1
    is_even = odd == 0
    pair = w + 1 - 2 * odd
    has_one = jnp.logical_or(is_even, w + 1 < wides)
    has_two = w + 2 < wides
    gives_two = w >= 2
    below = q >= 1
    above = q + 1 < quads
    enter([
        (w >= 1, {"wide": w - 1}), (gives_two, {"wide": w - 2}),
        (w + 1 < wides, {"wide": w + 1}), (has_two, {"wide": w + 2}),
        (below, {"quad": q - 1}), (above, {"quad": q + 1}),
    ])

    def columns(c):
        return pl.ds(c * chunk_width, chunk_width)

    def held(step, c):
        return pool.at[pl.ds(step * owned, owned), pl.ds(EDGE, planes), columns(c)]

    def corner_copy(step):
        return remote(
            corner_in, corner.at[step], corner_send.at[step - 1], corner_recv.at[step - 1],
            {"wide": w - step},
        )

    def own_to_two(c):
        return remote(
            orb.at[:, :, columns(c)], held(2, c), send_two.at[c], recv_two.at[c],
            {"wide": w - 2},
        )

    def own_to_pair(c):
        return remote(
            orb.at[:, :, columns(c)], held(1, c), send_one.at[c], recv_one.at[c],
            {"wide": pair},
        )

    def two_to_pair(c):
        return remote(held(2, c), held(1, c), send_one.at[c], recv_one.at[c], {"wide": pair})

    def own_edge(up):
        if up:
            return remote(
                orb.at[:, pl.ds(planes - EDGE, EDGE)],
                pool.at[pl.ds(0, owned), pl.ds(0, EDGE)],
                own_send.at[1], own_recv.at[1], {"quad": q + 1},
            )
        return remote(
            orb.at[:, pl.ds(0, EDGE)],
            pool.at[pl.ds(0, owned), pl.ds(EDGE + planes, EDGE)],
            own_send.at[0], own_recv.at[0], {"quad": q - 1},
        )

    def edge(step, up, c):
        rows = pl.ds(step * owned, owned)
        if up:
            src, dst, to = planes, 0, q + 1
        else:
            src, dst, to = EDGE, EDGE + planes, q - 1
        return remote(
            pool.at[rows, pl.ds(src, EDGE), columns(c)],
            pool.at[rows, pl.ds(dst, EDGE), columns(c)],
            edge_send.at[step - 1, int(up), c], edge_recv.at[step - 1, int(up), c],
            {"quad": to},
        )

    own_copy = pltpu.make_async_copy(
        orb, pool.at[pl.ds(0, owned), pl.ds(EDGE, planes)], local_sem.at[0]
    )
    corner_copy_own = pltpu.make_async_copy(corner_in, corner.at[0], local_sem.at[1])
    for step in (1, 2):
        @pl.when(w >= step)
        def _(step=step):
            corner_copy(step).start()
    own_copy.start()
    corner_copy_own.start()

    def pass_edges(step, c):
        @pl.when(below)
        def _():
            edge(step, False, c).start()

        @pl.when(above)
        def _():
            edge(step, True, c).start()

    for step in range(CHUNKS + 2 * AHEAD):
        if step < CHUNKS:
            if step >= AHEAD:
                @pl.when(gives_two)
                def _(c=step - AHEAD):
                    own_to_two(c).wait_send()

                @pl.when(is_odd)
                def _(c=step - AHEAD):
                    own_to_pair(c).wait_send()

            @pl.when(gives_two)
            def _(c=step):
                own_to_two(c).start()

            @pl.when(is_odd)
            def _(c=step):
                own_to_pair(c).start()
        if step == 0:
            @pl.when(below)
            def _():
                own_edge(False).start()

            @pl.when(above)
            def _():
                own_edge(True).start()
        if 0 <= step - AHEAD < CHUNKS:
            @pl.when(has_two)
            def _(c=step - AHEAD):
                own_to_two(c).wait_recv()

                @pl.when(is_even)
                def _():
                    two_to_pair(c).start()
                pass_edges(2, c)
        if 0 <= step - 2 * AHEAD < CHUNKS:
            @pl.when(has_one)
            def _(c=step - 2 * AHEAD):
                own_to_pair(c).wait_recv()
                pass_edges(1, c)

    for up, takes, gives in ((False, above, below), (True, below, above)):
        @pl.when(takes)
        def _(up=up):
            own_edge(up).wait_recv()

        @pl.when(gives)
        def _(up=up):
            own_edge(up).wait_send()
        for step, have in ((2, has_two), (1, has_one)):
            for c in range(CHUNKS):
                @pl.when(jnp.logical_and(takes, have))
                def _(up=up, step=step, c=c):
                    edge(step, up, c).wait_recv()

                @pl.when(jnp.logical_and(gives, have))
                def _(up=up, step=step, c=c):
                    edge(step, up, c).wait_send()
    for step in (1, 2):
        @pl.when(w + step < wides)
        def _(step=step):
            corner_copy(step).wait_recv()

        @pl.when(w >= step)
        def _(step=step):
            corner_copy(step).wait_send()
    for c in range(CHUNKS):
        if c >= CHUNKS - AHEAD:
            @pl.when(gives_two)
            def _(c=c):
                own_to_two(c).wait_send()

            @pl.when(is_odd)
            def _(c=c):
                own_to_pair(c).wait_send()

        @pl.when(jnp.logical_and(is_even, has_two))
        def _(c=c):
            two_to_pair(c).wait_send()
    own_copy.wait()
    corner_copy_own.wait()


def exchange_kernel(
    quads, slots, pool, corner_s, table, seg, dens, moved, pot_a, pot_b, final, prod,
):
    total_orbs, wide_rows, flat = pool.shape
    owned = total_orbs // 3
    planes = wide_rows - 2 * EDGE
    tiles = flat // LANES
    rows_y = flat // BZ
    w = lax.axis_index("wide")
    q = lax.axis_index("quad")

    lane = lax.broadcasted_iota(jnp.int32, (wide_rows, LANES), 1)
    zpos = lax.rem(lane, BZ)
    ylow = lane // BZ
    plane = lax.broadcasted_iota(jnp.int32, (wide_rows, LANES), 0) + (q * planes - EDGE)
    in_box = (plane >= 0) & (plane < quads * planes)

    def slot_facts(s):
        left = s % owned
        right = jnp.clip(corner_s[0, owned, s] - w * owned, 0, 3 * owned - 1)
        live = corner_s[0, owned + 1, s] != 0
        who, which = right // owned, lax.rem(right, owned)
        dy = corner_s[who, which, 0] - corner_s[0, left, 0]
        dz = corner_s[who, which, 1] - corner_s[0, left, 1]
        dy = jnp.clip(jnp.where(live, dy, 0), -SPAN, SPAN)
        dz = jnp.clip(jnp.where(live, dz, 0), -SPAN, SPAN)
        return left, right, live, dy, dz

    def mover(dy, dz, ok, rows):
        by = dy * BZ + dz
        whole = by >> 7
        rest = by & (LANES - 1)
        near_part = lane[:rows] < LANES - rest
        zfrom = zpos[:rows] - dz
        keep_z = (zfrom >= 0) & (zfrom < BZ) & ok
        yfrom = ylow[:rows] - dy

        def move(load, r):
            here = load(jnp.clip(r - whole, 0, tiles - 1))
            before = load(jnp.clip(r - whole - 1, 0, tiles - 1))
            turned = pltpu.roll(jnp.where(near_part, here, before), rest, 1)
            source = yfrom + 2 * r
            keep = keep_z & (source >= 0) & (source < rows_y)
            return jnp.where(keep, turned, 0.0)

        return move

    def column(t):
        return pl.ds(pl.multiple_of(t * LANES, LANES), LANES)

    half = tiles // 2
    factor = table[LANES:LANES + 8]

    bf16, f32 = jnp.bfloat16, jnp.float32
    fine = table[0:LANES]
    coarse = fine.astype(bf16)
    rest = (fine - coarse.astype(f32)).astype(bf16)
    both = jnp.concatenate([coarse, rest], axis=1)

    def transform(rows):
        high = rows.astype(bf16)
        low = (rows - high.astype(f32)).astype(bf16)
        total = jnp.dot(high, both, preferred_element_type=f32)
        return total[:, :LANES] + (
            total[:, LANES:] + jnp.dot(low, coarse, preferred_element_type=f32)
        )

    def regroup(a, b):
        low = lane[:a.shape[0]] < BZ
        return (
            jnp.where(low, a, pltpu.roll(b, BZ, 1)), jnp.where(low, pltpu.roll(a, BZ, 1), b)
        )

    def guard(field):
        rows = pl.ds(LOW - EDGE, wide_rows)
        field[0, rows] = jnp.where(lane >= BZ, pltpu.roll(field[tiles, rows], BZ, 1), 0.0)
        field[tiles + 1, rows] = jnp.where(lane < BZ, pltpu.roll(field[1, rows], BZ, 1), 0.0)

    facts = [slot_facts(s) for s in range(slots)]
    for s in range(slots):
        left, right, live, dy, dz = facts[s]
        move = mover(dy, dz, live, wide_rows)

        @pl.when(live)
        def _(s=s, left=left, right=right, move=move):
            def two_tiles(i, carry):
                parts = []
                for r in (i, i + half):
                    there = move(lambda t: pool[right, :, column(t)], r)
                    moved[s, r] = there[EDGE:EDGE + planes]
                    parts.append(jnp.where(in_box, there * pool[left, :, column(r)], 0.0))
                first, second = regroup(*parts)
                dens[s, 2 * i + 1, LOW - EDGE:LOW + planes + EDGE] = first
                dens[s, 2 * i + 2, LOW - EDGE:LOW + planes + EDGE] = second
                return carry

            lax.fori_loop(0, half, two_tiles, 0, unroll=4)

            def to_waves(i, carry):
                at = (s, pl.ds(1 + i * BLOCK, BLOCK), pl.ds(LOW - EDGE, wide_rows))
                rows = dens[at].reshape(BLOCK * wide_rows, LANES)
                dens[at] = transform(rows).reshape(BLOCK, wide_rows, LANES)
                return carry

            lax.fori_loop(0, tiles // BLOCK, to_waves, 0)
            guard(dens.at[s])

        @pl.when(jnp.logical_not(live))
        def _(s=s):
            def clear(r, carry):
                for field in (moved, final, prod):
                    field[s, r] = jnp.zeros((planes, LANES), jnp.float32)
                return carry

            lax.fori_loop(0, tiles, clear, 0, unroll=4)

    weights = sweep_weights()
    pots = (pot_a, pot_b)
    nothing = jnp.minimum(w, 0)

    def one_slot(s, carry):
        for k in range(1, SWEEPS):
            gain = weights[k] / 6.5
            if k == 1:
                read = lambda t, first, size: dens[s, t, pl.ds(first, size)]
            else:
                read = lambda t, first, size, k=k: pots[k % 2][t, pl.ds(first, size)]
            last = k == SWEEPS - 1

            first, size = (LOW, planes) if last else (LOW - EDGE, wide_rows)
            if k == 1:
                start = weights[0] / 6.5
                keep = (1.0 - weights[1]) * start + gain + gain * start * factor
                gain = gain * start
            else:
                keep = (1.0 - weights[k]) + gain * factor
            keep = jnp.concatenate([keep] * (size // 8))

            def some_tiles(i, inner, k=k, gain=gain, read=read, last=last, keep=keep, first=first, size=size):
                r = i * GROUP
                next_row = first + 1 + nothing
                last_row = first - 1 + nothing
                here = [read(r + g, first, size) for g in range(GROUP + 2)]
                news = []
                for g in range(GROUP):
                    total = read(r + g + 1, next_row, size) + read(r + g + 1, last_row, size)
                    total = total + (here[g] + here[g + 2])
                    if k > 1:
                        total = total + dens[s, r + g + 1, pl.ds(first, size)]
                    new = keep * here[g + 1] + gain * total
                    if not last:
                        new = jnp.where(in_box, new, 0.0)
                    news.append(new)
                for g in range(GROUP):
                    pots[(k + 1) % 2][r + g + 1, pl.ds(first, size)] = news[g]
                return inner

            lax.fori_loop(0, tiles // GROUP, some_tiles, 0, unroll=2)
            if not last:
                guard(pots[(k + 1) % 2])

        def to_cells(i, inner):
            at = (pl.ds(1 + i * BLOCK, BLOCK), pl.ds(LOW, planes))
            rows = pots[SWEEPS % 2][at].reshape(BLOCK * planes, LANES)
            cells = transform(rows).reshape(BLOCK, planes, LANES)
            for g in range(0, BLOCK, 2):
                t = i * (BLOCK // 2) + g // 2
                for place, value in zip((t, t + half), regroup(cells[g], cells[g + 1])):
                    final[s, place] = value
                    own = pool[lax.rem(s, owned), EDGE:EDGE + planes, column(place)]
                    prod[s, place] = value * own
            return inner

        lax.fori_loop(0, tiles // BLOCK, to_cells, 0)
        return carry

    def live_slot(s, carry):
        @pl.when(corner_s[0, owned + 1, s] != 0)
        def _():
            one_slot(s, 0)
        return carry

    lax.fori_loop(0, slots, live_slot, 0)

    backs = [mover(-dy, -dz, live, planes) for left, right, live, dy, dz in facts]

    def terms(r, carry):
        total = [jnp.zeros((planes, LANES), jnp.float32) for o in range(3 * owned)]
        for s in range(slots):
            left, right = facts[s][:2]
            total[left] = total[left] + final[s, r] * moved[s, r]
            term = backs[s](lambda t: prod[s, t], r)
            for o in range(left + 1, min(left + 1 + REACH, 3 * owned)):
                total[o] = total[o] + jnp.where(right == o, term, 0.0)
        for o in range(3 * owned):
            seg[o, :, column(r)] = total[o]
        return carry

    lax.fori_loop(0, tiles, terms, 0, unroll=4)


def return_kernel(
    wides, seg, out, own, two, from_pair, from_two,
    local_sem, send_one, recv_one, send_two, recv_two,
):
    owned, planes, flat = out.shape
    chunk_width = flat // CHUNKS
    w = lax.axis_index("wide")
    odd = lax.rem(w, 2)
    is_odd = odd == 1
    is_even = odd == 0
    pair = w + 1 - 2 * odd
    has_two = w + 2 < wides
    takes_two = w >= 2
    takes_pair = jnp.logical_or(is_odd, has_two)
    even_two = jnp.logical_and(is_even, has_two)

    own_copy = pltpu.make_async_copy(seg.at[pl.ds(0, owned)], own, local_sem.at[0])
    two_copy = pltpu.make_async_copy(seg.at[pl.ds(2 * owned, owned)], two, local_sem.at[1])
    own_copy.start()
    two_copy.start()
    enter([
        (w >= 0, {"wide": pair}), (takes_two, {"wide": w - 2}), (has_two, {"wide": w + 2}),
    ])

    def columns(c):
        return pl.ds(c * chunk_width, chunk_width)

    def back_to_pair(c):
        return remote(
            seg.at[pl.ds(owned, owned), :, columns(c)], from_pair.at[:, :, columns(c)],
            send_one.at[c], recv_one.at[c], {"wide": pair},
        )

    def back_to_two(c):
        return remote(
            two.at[:, :, columns(c)], from_two.at[:, :, columns(c)],
            send_two.at[c], recv_two.at[c], {"wide": w + 2},
        )

    two_copy.wait()
    for c in range(CHUNKS):
        if c >= AHEAD:
            @pl.when(jnp.logical_and(is_odd, has_two))
            def _(c=c - AHEAD):
                back_to_pair(c).wait_send()
                back_to_two(c).wait_send()

        @pl.when(jnp.logical_and(is_odd, has_two))
        def _(c=c):
            back_to_pair(c).start()
            back_to_two(c).start()

        @pl.when(jnp.logical_and(is_even, jnp.logical_not(has_two)))
        def _(c=c):
            back_to_pair(c).start()
    for c in range(CHUNKS):
        @pl.when(takes_pair)
        def _(c=c):
            back_to_pair(c).wait_recv()

        @pl.when(even_two)
        def _(c=c):
            two[:, :, columns(c)] += from_pair[:, :, columns(c)]
            back_to_two(c).start()
            back_to_pair(c).start()
    own_copy.wait()
    for c in range(CHUNKS):
        out[:, :, columns(c)] = own[:, :, columns(c)]

        @pl.when(is_odd)
        def _(c=c):
            out[:, :, columns(c)] += from_pair[:, :, columns(c)]

        @pl.when(takes_two)
        def _(c=c):
            back_to_two(c).wait_recv()
            out[:, :, columns(c)] += from_two[:, :, columns(c)]
    for c in range(CHUNKS):
        @pl.when(is_even)
        def _(c=c):
            back_to_pair(c).wait_send()

        @pl.when(even_two)
        def _(c=c):
            back_to_two(c).wait_send()
        if c >= CHUNKS - AHEAD:
            @pl.when(jnp.logical_and(is_odd, has_two))
            def _(c=c):
                back_to_pair(c).wait_send()
                back_to_two(c).wait_send()


def per_device(wides, quads, orbitals, corners, pair_partner, pair_live):
    owned, planes, flat = orbitals.shape
    slots = pair_partner.shape[0]
    tiles = flat // LANES
    field_rows = planes + 2 * LOW
    corner_block = jnp.pad(corners, ((0, 8 - owned), (0, LANES - corners.shape[1])))
    for row, facts in ((owned, pair_partner), (owned + 1, pair_live)):
        corner_block += jnp.pad(facts[None], ((row, 7 - row), (0, LANES - slots)))
    f32 = jnp.float32
    dma = pltpu.SemaphoreType.DMA
    vmem = pl.BlockSpec(memory_space=pltpu.VMEM)
    smem = pl.BlockSpec(memory_space=pltpu.SMEM)
    anywhere = pl.BlockSpec(memory_space=pl.ANY)
    limit = 32 * 1024 * 1024
    pool, pool_corner = pl.pallas_call(
        functools.partial(gather_kernel, wides, quads),
        out_shape=(
            jax.ShapeDtypeStruct((3 * owned, planes + 2 * EDGE, flat), f32),
            jax.ShapeDtypeStruct((3, 8, LANES), jnp.int32),
        ),
        in_specs=[pl.BlockSpec(memory_space=pltpu.HBM), anywhere],
        out_specs=(anywhere, anywhere),
        scratch_shapes=[
            dma((2,)), dma((2,)), dma((2,)),
            dma((CHUNKS,)), dma((CHUNKS,)), dma((CHUNKS,)), dma((CHUNKS,)),
            dma((2, 2, CHUNKS)), dma((2, 2, CHUNKS)), dma((2,)), dma((2,)),
        ],
        compiler_params=pltpu.CompilerParams(
            collective_id=0, has_side_effects=True, vmem_limit_bytes=limit
        ),
        name="gather",
    )(orbitals, corner_block)
    seg = pl.pallas_call(
        functools.partial(exchange_kernel, quads, slots),
        out_shape=jax.ShapeDtypeStruct((3 * owned, planes, flat), f32),
        in_specs=[vmem, smem, vmem],
        out_specs=vmem,
        scratch_shapes=[
            pltpu.VMEM((slots, tiles + 2, field_rows, LANES), f32),
            pltpu.VMEM((slots, tiles, planes, LANES), f32),
            pltpu.VMEM((tiles + 2, field_rows, LANES), f32),
            pltpu.VMEM((tiles + 2, field_rows, LANES), f32),
            pltpu.VMEM((slots, tiles, planes, LANES), f32),
            pltpu.VMEM((slots, tiles, planes, LANES), f32),
        ],
        compiler_params=pltpu.CompilerParams(vmem_limit_bytes=limit),
        name="exchange",
    )(pool, pool_corner, jnp.asarray(sine_table()))
    return pl.pallas_call(
        functools.partial(return_kernel, wides),
        out_shape=jax.ShapeDtypeStruct(orbitals.shape, f32),
        in_specs=[anywhere],
        out_specs=vmem,
        scratch_shapes=[
            pltpu.VMEM((owned, planes, flat), f32),
            pltpu.VMEM((owned, planes, flat), f32),
            pltpu.VMEM((owned, planes, flat), f32),
            pltpu.VMEM((owned, planes, flat), f32),
            dma((2,)), dma((CHUNKS,)), dma((CHUNKS,)), dma((CHUNKS,)), dma((CHUNKS,)),
        ],
        compiler_params=pltpu.CompilerParams(
            collective_id=1, has_side_effects=True, vmem_limit_bytes=limit
        ),
        name="give_back",
    )(seg)


def solution(mesh):
    in_specs = (P("wide", "quad", None), P("wide", None), P("wide"), P("wide"))
    out_specs = P("wide", "quad", None)
    body = functools.partial(per_device, mesh.shape["wide"], mesh.shape["quad"])
    return jax.shard_map(
        body, mesh=mesh, in_specs=in_specs, out_specs=out_specs, check_vma=False
    )
```
